128 devices in a mesh: pb: 8 (over x, y_lo), pa: 16 (over z, y_hi, core).
Axes of the slice: x: 4, y: 4 (y_hi: 2, y_lo: 2; y = y_hi * 2 + y_lo), z: 4, core: 2. Of those that a mesh axis runs over, the one named last changes fastest.
Arguments:
- query_cache: bfloat16 [8, 512, 4096], P('pb', 'pa'), may hold values from -0.4 to 0.4
- passage_cache: bfloat16 [16, 256, 4096], P('pa', 'pb'), may hold values from -0.4 to 0.4
- positive: int32 [8, 512], P('pb', 'pa'), may hold values from 0 to 4095
- query_tokens: bfloat16 [8, 16, 128, 4096], P('pb', 'pa'), may hold values from -6 to 6
- passage_tokens: bfloat16 [16, 8, 768, 4096], P('pa', 'pb'), may hold values from -6 to 6
- query_lengths: int32 [8, 16, 4], P('pb', 'pa'), may hold values from 1 to 64, 128 in all within a row
- passage_lengths: int32 [16, 8, 2], P('pa', 'pb'), may hold values from 1 to 512, 768 in all within a row
- norm_gain: bfloat16 [4096], P(('pb', 'pa')), may hold values from 0.099609375 to 1.8984375
- adapter_down: bfloat16 [4096, 512], P(('pb', 'pa')), may hold values from -0.09375 to 0.09375
- adapter_up: bfloat16 [512, 4096], P(('pb', 'pa')), may hold values from -0.25 to 0.25
Outputs:
- query_grad: bfloat16 [8, 512, 4096], P('pb', 'pa')
- passage_grad: bfloat16 [16, 256, 4096], P('pa', 'pb')
- down_grad: float32 [4096, 512], P(('pb', 'pa'))
- up_grad: float32 [512, 4096], P(('pb', 'pa'))
- gain_grad: float32 [4096], P(('pb', 'pa'))
The draws below stay inside these ranges and needn't reach their ends.
All inputs are finite; a program needn't handle non-finite values.
Results may differ from the reference program's by a relative error of at most 0.028.
Values may be sent and summed in bfloat16 or wider, within the bound.
No kernel may reach another device: no remote copies, remote signals or barrier semaphores. Data moves between devices by JAX's collectives and lax.ppermute only.
A program may use at most 128 MiB of HBM per device.

```python
import math
import jax
import jax.numpy as jnp
import numpy as np
from jax import lax

D = 4096
R = 512
QROW = 32
PROW = 32
QCH = 4
PCH = 2
TQ = 128
TP = 768
QMAX = 64
PMAX = 512
QBLK = 512
PBLK = 256
NQ = 4096
NP = 4096
N_PB = 8
N_PA = 16


def aligned_rows(key):
    sign_key, size_key = jax.random.split(key)
    signs = jnp.where(jax.random.bernoulli(sign_key, 0.5, (8, D)), 1.0, -1.0).astype(jnp.float32)
    factor = jax.random.uniform(size_key, (8, D), jnp.float32, 0.9, 1.1)
    target_score = 120.0 + 200.0 / 7.0 * jnp.arange(8, dtype=jnp.float32)
    strength = jnp.sqrt(0.05 * target_score / D)
    return jnp.clip(signs * factor * strength[:, None], -0.4, 0.4)


def draw_query_cache(key, part):
    shared = aligned_rows(key)
    key = jax.random.fold_in(key, 11)
    first_key = jax.random.fold_in(key, 0)
    values = 0.05 * jnp.clip(jax.random.normal(first_key, (NQ, D), jnp.float32), -5.0, 5.0)
    selected_entries = jnp.arange(8, dtype=jnp.int32) * (NQ // 8)
    values = values.at[selected_entries].set(shared)
    return values.reshape(N_PB, QBLK, D).astype(jnp.bfloat16)


def draw_passage_cache(key, part):
    shared = aligned_rows(key)
    key = jax.random.fold_in(key, 23)
    first_key = jax.random.fold_in(key, 0)
    third_key = jax.random.fold_in(key, 2)
    values = 0.05 * jnp.clip(jax.random.normal(first_key, (NP, D), jnp.float32), -5.0, 5.0)
    selected_entries = jnp.arange(8, dtype=jnp.int32) * (NP // 8)
    noise = 0.005 * jnp.clip(jax.random.normal(third_key, (8, D), jnp.float32), -5.0, 5.0)
    values = values.at[selected_entries].set(shared)
    values = values.at[selected_entries + 1].set(jnp.clip(0.995 * shared + noise, -0.4, 0.4))
    return values.reshape(N_PA, PBLK, D).astype(jnp.bfloat16)


def plant(entries, rng, low, top_value):
    dims = entries.shape
    spot = [jax.random.randint(jax.random.fold_in(rng, axis), (), 0, dims[axis]) for axis in range(len(dims))]
    entries = entries.at[tuple(spot)].set(low)
    longest = dims.index(max(dims))
    spot[longest] = (spot[longest] + 1) % dims[longest]
    return entries.at[tuple(spot)].set(top_value)


def steps_of(own_key, extent, shards, least, high):
    def one(dim, shards_of):
        heights = jax.random.uniform(jax.random.fold_in(jax.random.fold_in(own_key, 6), dim), (shards_of,), jnp.float32, least / len(shards), high / len(shards))
        return jnp.repeat(jnp.exp(heights), extent[dim] // shards_of).reshape((-1,) + (1,) * (len(extent) - dim - 1))

    factor_of = one(*shards[0])
    for cut in shards[1:]:
        factor_of = factor_of * one(*cut)
    return factor_of


def profile(number_of, total, most, lean):
    portions = [(1 << 20) // math.isqrt(standing ** lean) + 1 for standing in range(2, number_of + 1)]
    spare, given = total - most - (number_of - 1), [1] * (number_of - 1)
    while spare > 0:
        candidates = [i for i in range(number_of - 1) if given[i] < most]
        mass, remaining = sum([portions[i] for i in candidates]), spare
        for i in candidates:
            addition = min(most - given[i], max(1, remaining * portions[i] // mass), spare)
            given[i] = given[i] + addition
            spare = spare - addition
    return np.array([most] + given)


def uneven(rng, number_of, total, most, lean):
    if number_of == 2:
        one = jax.random.randint(rng, (), max(1, total - most), min(most, total - 1) + 1)
        return jnp.stack([one, total - one])
    sizes = jnp.asarray(profile(number_of, total, most, lean), jnp.int32)
    couples = (number_of - 1) // 2
    donor, sink = sizes[1:1 + 2 * couples:2], sizes[2:2 + 2 * couples:2]
    margin = jnp.minimum(donor - 1, most - sink)
    passed = jax.random.randint(jax.random.fold_in(rng, 1), (couples,), 0, 1 << 20) % (margin + 1)
    sizes = sizes.at[1:1 + 2 * couples:2].set(donor - passed).at[2:2 + 2 * couples:2].set(sink + passed)
    return sizes[jax.random.permutation(jax.random.fold_in(rng, 2), number_of)]


def normal_values(key, dims, spread, reach, cuts=(), held_as=jnp.bfloat16):
    factor_of = steps_of(key, dims, cuts, -0.22, 0.18) if cuts else 1.0
    result = jax.random.normal(key, dims, jnp.float32) * spread * factor_of
    return jnp.minimum(jnp.maximum(result, -reach), reach).astype(held_as)


def setup_inputs(seed: int = 0) -> dict:
    splits = jax.random.split(jax.random.key(seed), 11)
    return {
        "query_cache": draw_query_cache(jax.random.fold_in(splits[10], 71), 0),
        "passage_cache": draw_passage_cache(jax.random.fold_in(splits[10], 71), 0),
        "positive": plant(jax.random.randint(splits[2], (N_PB, QBLK), 0, NP), jax.random.fold_in(splits[2], 1), 0, NP - 1).astype(jnp.int32),
        "query_tokens": normal_values(splits[3], (N_PB, N_PA, TQ, D), 1.0, 6.0, ((0, 8), (1, 16))),
        "passage_tokens": normal_values(splits[4], (N_PA, N_PB, TP, D), 1.0, 6.0, ((0, 16), (1, 8))),
        "query_lengths": jax.vmap(lambda own: uneven(own, QCH, TQ, QMAX, 1))(jax.random.split(splits[5], N_PB * N_PA)).reshape((N_PB, N_PA, QCH)).astype(jnp.int32),
        "passage_lengths": jax.vmap(lambda own: uneven(own, PCH, TP, PMAX, 1))(jax.random.split(splits[6], N_PA * N_PB)).reshape((N_PA, N_PB, PCH)).astype(jnp.int32),
        "norm_gain": jnp.clip(1.0 + 0.18 * jax.random.normal(splits[7], (D,), jnp.float32), 0.099609375, 1.8984375).astype(jnp.bfloat16),
        "adapter_down": normal_values(splits[8], (D, R), D ** -0.5, 0.09375, ((0, 128),)),
        "adapter_up": normal_values(splits[9], (R, D), R ** -0.5, 0.25, ((0, 128),)),
    }


logit_divisor = 0.05
epsilon = 1e-06

def gelu_grad(pre_act, upstream):
    values, pullback = jax.vjp(lambda v: jax.nn.gelu(v, approximate=True), pre_act)
    return pullback(upstream)[0]

def stretch_terms(tokens, lengths, emb_grads, gain, down, up):
    row_count = tokens.shape[0]
    seq_ends = jnp.cumsum(lengths).astype(jnp.int32)
    seq_starts = (seq_ends - lengths).astype(jnp.int32)
    position = jnp.arange(row_count, dtype=jnp.int32)[:, None]
    member = ((position >= seq_starts[None, :]) & (position < seq_ends[None, :])).astype(jnp.float32)
    scaled = emb_grads / lengths.astype(jnp.float32)[:, None]
    token_grad = jnp.dot(member, scaled, precision=lax.Precision.HIGHEST).astype(jnp.bfloat16)
    widened = tokens.astype(jnp.float32)
    inverse = lax.rsqrt(lax.optimization_barrier(jnp.mean(widened * widened, axis=1, keepdims=True)) + epsilon)
    normed = (widened * inverse * gain.astype(jnp.float32)[None, :]).astype(jnp.bfloat16)
    pre_act = jnp.dot(normed, down, preferred_element_type=jnp.float32)
    active = jax.nn.gelu(pre_act, approximate=True).astype(jnp.bfloat16)
    up_term = lax.dot_general(active, token_grad, (((0,), (0,)), ((), ())), preferred_element_type=jnp.float32)
    hidden_grad = lax.dot_general(token_grad, up, (((1,), (1,)), ((), ())), preferred_element_type=jnp.float32)
    inner_grad = gelu_grad(pre_act, hidden_grad).astype(jnp.bfloat16)
    down_term = lax.dot_general(normed, inner_grad, (((0,), (0,)), ((), ())), preferred_element_type=jnp.float32)
    normed_grad = lax.dot_general(inner_grad, down, (((1,), (1,)), ((), ())), preferred_element_type=jnp.float32)
    gain_term = lax.optimization_barrier(jnp.sum(normed_grad * widened * inverse, axis=0))
    return (gain_term, down_term, up_term)

def reference(query_cache, passage_cache, positive, query_tokens, passage_tokens, query_lengths, passage_lengths, norm_gain, adapter_down, adapter_up):
    question_group = query_cache.reshape(NQ, D)
    document_group = passage_cache.reshape(NP, D)
    similarity_grid = lax.dot_general(question_group, document_group, (((1,), (1,)), ((), ())), preferred_element_type=jnp.float32) * (1.0 / logit_divisor)
    row_top = lax.optimization_barrier(jnp.max(similarity_grid, axis=1, keepdims=True))
    weights = jnp.exp(similarity_grid - row_top)
    softmax_w = weights / lax.optimization_barrier(jnp.sum(weights, axis=1, keepdims=True))
    target = (positive.reshape(NQ)[:, None] == jnp.arange(NP, dtype=jnp.int32)[None, :]).astype(jnp.float32)
    similarity_link = (softmax_w - target).astype(jnp.bfloat16)
    query_total = jnp.zeros((NQ, D), jnp.float32)
    for shard_idx in range(N_PA):
        target_width_count = slice(shard_idx * PBLK, (shard_idx + 1) * PBLK)
        piece_objective_amount = jnp.dot(similarity_link[:, target_width_count], document_group[target_width_count], preferred_element_type=jnp.float32) * (1.0 / logit_divisor)
        query_total = query_total + piece_objective_amount.astype(jnp.bfloat16).astype(jnp.float32)
    passage_total = jnp.zeros((NP, D), jnp.float32)
    for shard_idx in range(N_PB):
        source_height_count = slice(shard_idx * QBLK, (shard_idx + 1) * QBLK)
        piece_objective_amount = lax.dot_general(similarity_link[source_height_count], question_group[source_height_count], (((0,), (0,)), ((), ())), preferred_element_type=jnp.float32) * (1.0 / logit_divisor)
        passage_total = passage_total + piece_objective_amount.astype(jnp.bfloat16).astype(jnp.float32)
    query_grad = query_total.astype(jnp.bfloat16).reshape(N_PB, QBLK, D)
    passage_grad = passage_total.astype(jnp.bfloat16).reshape(N_PA, PBLK, D)
    query_stretch = query_grad.reshape(N_PB, N_PA, QROW, D)[:, :, :QCH].astype(jnp.float32)
    passage_stretch = jnp.swapaxes(passage_grad.reshape(N_PA, N_PB, PROW, D)[:, :, :PCH], 0, 1).astype(jnp.float32)
    slot_tokens = jnp.concatenate([query_tokens, jnp.swapaxes(passage_tokens, 0, 1)], axis=2).reshape(N_PB * N_PA, TQ + TP, D)
    slot_lengths = jnp.concatenate([query_lengths, jnp.swapaxes(passage_lengths, 0, 1)], axis=2).reshape(N_PB * N_PA, QCH + PCH).astype(jnp.int32)
    slot_grads = jnp.concatenate([query_stretch, passage_stretch], axis=2).reshape(N_PB * N_PA, QCH + PCH, D)

    def accumulate(running, device_item):
        tokens, lengths, emb_grads = device_item
        partials = stretch_terms(tokens, lengths, emb_grads, norm_gain, adapter_down, adapter_up)
        return ((running[0] + partials[0], running[1] + partials[1], running[2] + partials[2]), None)
    start_state = (jnp.zeros((D,), jnp.float32), jnp.zeros((D, R), jnp.float32), jnp.zeros((R, D), jnp.float32))
    sums, unused = lax.scan(accumulate, start_state, (slot_tokens, slot_lengths, slot_grads))
    return (query_grad, passage_grad, sums[1], sums[2], sums[0])
```

```python
import jax
import jax.numpy as jnp
from jax import lax
from jax.sharding import Mesh, PartitionSpec as P

scale = 1.0 / 0.05
epsilon = 1e-06
bf16 = jnp.bfloat16
f32 = jnp.float32
chips = ("x", "yl", "z", "yh")
everyone = ("x", "yl", "z", "yh", "c")
swap2 = [(0, 1), (1, 0)]


def shift(value, axis, step, size):
    return lax.ppermute(value, axis, [(i, (i + step) % size) for i in range(size)])


def gather_pair(block, ring, size, pair):
    other = lax.ppermute(block, pair, swap2)
    own_row = [block] + [shift(block, ring, k, size) for k in range(1, size)]
    other_row = [other] + [shift(other, ring, k, size) for k in range(1, size)]
    return jnp.concatenate([b for two in zip(own_row, other_row) for b in two], axis=0)


def scatter_pair(part, ring, size, pair):
    rows = part.shape[0] // size
    total = part[:rows].astype(f32)
    for k in range(1, size):
        total = total + shift(part[k * rows : (k + 1) * rows], ring, size - k, size).astype(f32)
    half = rows // 2
    other = lax.ppermute(total[half:].astype(bf16), pair, swap2)
    return (total[:half] + other.astype(f32)).astype(bf16)


def spread(block, axes, count):
    return lax.all_to_all(jnp.broadcast_to(block[None], (count,) + block.shape), axes, 0, 0)


def per_device(sizes, query_cache, passage_cache, positive, query_tokens, passage_tokens,
               query_lengths, passage_lengths, norm_gain, adapter_down, adapter_up):
    nx, nyl, nz, nyh, nc = sizes
    n_chips = nx * nyl * nz * nyh
    n_all = n_chips * nc
    x_i, yl_i, z_i, yh_i, c_i = (lax.axis_index(a) for a in everyone)
    own_queries, own_passages = query_cache[0], passage_cache[0]
    width = own_queries.shape[1]
    qrow, prow = own_queries.shape[0], own_passages.shape[0]

    queries = gather_pair(own_queries, "z", nz, "yh")
    mine_p = gather_pair(own_passages, "x", nx, "yl")

    gain = norm_gain.astype(f32)
    gained_down = (adapter_down.astype(f32) * gain[:, None]).astype(bf16)
    down_half = spread(gained_down, chips, n_chips)
    down_other = lax.ppermute(down_half, "c", swap2)
    first_core = c_i == 0
    down_full = jnp.stack(
        [jnp.where(first_core, down_half, down_other), jnp.where(first_core, down_other, down_half)], axis=1
    ).reshape(width, -1)

    other_p = lax.ppermute(mine_p, "c", swap2)
    passages = jnp.concatenate([mine_p, other_p], axis=0)

    scores = lax.dot_general(queries, passages, (((1,), (1,)), ((), ())), preferred_element_type=f32) * scale
    local_top = jnp.max(scores, axis=1)
    local_sum = jnp.sum(jnp.exp(scores - local_top[:, None]), axis=1)

    m_i = z_i * nyh + yh_i
    groups = nz * nyh
    step = jnp.arange(groups, dtype=jnp.int32)
    owner = lax.rem(z_i - step // nyh + nz, nz) * nyh + lax.rem(yh_i - step % nyh + nyh, nyh)
    pick = owner[:, None] == step[None, :]

    def to_owner(v):
        return jnp.sum(jnp.where(pick[:, :, None], v.reshape(groups, 1, qrow), 0), axis=0)

    def to_step(v):
        return jnp.sum(jnp.where(pick[:, :, None], v.reshape(1, groups, qrow), 0), axis=1).reshape(-1)

    packet = jnp.concatenate(
        [to_owner(local_top).reshape(-1), to_owner(local_sum).reshape(-1), positive[0].astype(f32)]
    )
    packet = jnp.pad(packet, (0, -packet.shape[0] % 128))
    stats = spread(packet, ("z", "yh"), groups)
    n_q = groups * qrow
    tops, sums = stats[:, :n_q], stats[:, n_q : 2 * n_q]
    row_top = jnp.max(tops, axis=0)
    row_sum = jnp.sum(sums * jnp.exp(tops - row_top[None, :]), axis=0)
    row_top, row_sum = to_step(row_top), to_step(row_sum)
    target = to_step(stats[:, 2 * n_q : 2 * n_q + qrow])

    core_step = jnp.arange(nc, dtype=jnp.int32)[:, None, None, None]
    x_step = jnp.arange(nx, dtype=jnp.int32)[None, :, None, None]
    yl_step = jnp.arange(nyl, dtype=jnp.int32)[None, None, :, None]
    lane = jnp.arange(prow, dtype=jnp.int32)[None, None, None, :]
    a_of = m_i * nc + lax.rem(c_i + core_step, nc)
    b_of = lax.rem(x_i - x_step + nx, nx) * nyl + lax.rem(yl_i - yl_step + nyl, nyl)
    columns = (a_of * (nx * nyl * prow) + b_of * prow + lane).reshape(-1)

    soft = jnp.exp(scores - row_top[:, None]) / row_sum[:, None]
    hit = (target.astype(jnp.int32)[:, None] == columns[None, :]).astype(f32)
    coupling = (soft - hit).astype(bf16)

    p_part = (
        lax.dot_general(coupling, queries, (((0,), (0,)), ((), ())), preferred_element_type=f32) * scale
    ).astype(bf16)
    q_part = (jnp.dot(coupling, passages, preferred_element_type=f32) * scale).astype(bf16)
    half = p_part.shape[0] // 2
    p_pair = (p_part[:half].astype(f32) + lax.ppermute(p_part[half:], "c", swap2).astype(f32)).astype(bf16)
    query_grad = scatter_pair(q_part, "z", nz, "yh")
    passage_grad = scatter_pair(p_pair, "x", nx, "yl")

    tokens = jnp.concatenate([query_tokens[0, 0], passage_tokens[0, 0]], axis=0)
    lengths = jnp.concatenate([query_lengths[0, 0], passage_lengths[0, 0]], axis=0)
    n_seq = lengths.shape[0]
    pad = -n_seq % 8
    rows = tokens.shape[0]
    ends = jnp.cumsum(lengths)
    starts = ends - lengths
    position = jnp.arange(rows, dtype=jnp.int32)[:, None]
    member = (position >= starts[None, :]) & (position < ends[None, :])
    member = jnp.pad(member, ((0, 0), (0, pad))).astype(f32)
    widened = tokens.astype(f32)
    inverse = lax.rsqrt(jnp.mean(widened * widened, axis=1, keepdims=True) + epsilon)
    pre_act = jnp.dot(tokens, down_full, preferred_element_type=f32) * inverse
    active, slope = jax.jvp(lambda v: jax.nn.gelu(v, approximate=True), (pre_act,), (jnp.ones_like(pre_act),))
    active_sums = lax.dot_general(
        member.astype(bf16), active.astype(bf16), (((0,), (0,)), ((), ())), preferred_element_type=f32
    ).astype(bf16)
    all_sums = spread(active_sums, everyone, n_all)

    up_half = spread(adapter_up, chips, n_chips)
    up_other = lax.ppermute(up_half, "c", swap2)
    r_own = adapter_up.shape[0]

    emb_grads = jnp.concatenate(
        [query_grad[: query_lengths.shape[-1]], passage_grad[: passage_lengths.shape[-1]]], axis=0
    ).astype(f32)
    seq_grads = (emb_grads / lengths.astype(f32)[:, None]).astype(bf16)
    seq_grads = jnp.pad(seq_grads, ((0, pad), (0, 0)))
    n_seq8 = n_seq + pad

    col_block = width // n_all
    grad_cols = lax.all_to_all(
        seq_grads.reshape(n_seq8, n_all, col_block).transpose(1, 0, 2), everyone, 0, 0
    )
    up_cols = lax.dot_general(
        all_sums.reshape(n_all * n_seq8, -1),
        grad_cols.reshape(n_all * n_seq8, col_block),
        (((0,), (0,)), ((), ())),
        preferred_element_type=f32,
    )
    up_rows = lax.all_to_all(up_cols.reshape(n_all, r_own, col_block), everyone, 0, 0)
    up_grad = up_rows.transpose(1, 0, 2).reshape(r_own, width)

    def project(block):
        return lax.dot_general(
            seq_grads, block.reshape(n_chips * r_own, width), (((1,), (1,)), ((), ())), preferred_element_type=f32
        ).reshape(n_seq8, n_chips, r_own)

    h_own, h_other = project(up_half), project(up_other)
    hidden = jnp.stack(
        [jnp.where(first_core, h_own, h_other), jnp.where(first_core, h_other, h_own)], axis=2
    ).reshape(n_seq8, -1)
    hidden_rows = jnp.dot(member, hidden, precision=lax.Precision.HIGHEST)
    inner = (slope * hidden_rows * inverse).astype(bf16)
    down_part = lax.dot_general(tokens, inner, (((0,), (0,)), ((), ())), preferred_element_type=f32).astype(bf16)

    d_own = adapter_down.shape[0]
    by_core = down_part.reshape(n_chips, nc, d_own, -1)
    keep = jnp.where(first_core, by_core[:, 0], by_core[:, 1])
    give = jnp.where(first_core, by_core[:, 1], by_core[:, 0])
    chip_sum = (keep.astype(f32) + lax.ppermute(give, "c", swap2).astype(f32)).astype(bf16)
    ungained = jnp.sum(lax.all_to_all(chip_sum, chips, 0, 0).astype(f32), axis=0)
    down_grad = ungained * gain[:, None]
    gain_grad = jnp.sum(ungained * adapter_down.astype(f32), axis=1)
    return (query_grad[None], passage_grad[None], down_grad, up_grad, gain_grad)


def solution(mesh):
    nyl, nyh, nc = 2, 2, 2
    nx, nz = mesh.shape["pb"] // nyl, mesh.shape["pa"] // (nyh * nc)
    sizes = (nx, nyl, nz, nyh, nc)
    fine = Mesh(mesh.devices.reshape(sizes), everyone)
    pb, pa = ("x", "yl"), ("z", "yh", "c")
    in_specs = (
        P(pb, pa, None),
        P(pa, pb, None),
        P(pb, pa),
        P(pb, pa, None, None),
        P(pa, pb, None, None),
        P(pb, pa, None),
        P(pa, pb, None),
        P(everyone),
        P(everyone, None),
        P(everyone, None),
    )
    out_specs = (P(pb, pa, None), P(pa, pb, None), P(everyone, None), P(everyone, None), P(everyone))

    def body(*args):
        return per_device(sizes, *args)

    return jax.shard_map(body, mesh=fine, in_specs=in_specs, out_specs=out_specs, check_vma=False)
```

```python
import jax
import jax.numpy as jnp
from jax import lax
from jax.sharding import Mesh, PartitionSpec as P

scale = 1.0 / 0.05
epsilon = 1e-06
bf16 = jnp.bfloat16
f32 = jnp.float32
everyone = ("x", "yl", "z", "yh", "c")
swap2 = [(0, 1), (1, 0)]
barrier = lax.optimization_barrier


def shift(value, axis, step, size):
    return lax.ppermute(value, axis, [(i, (i + step) % size) for i in range(size)])


def swap(value, axis):
    return lax.ppermute(value, axis, swap2)


def ring_parts(block, ring, size):
    return [block] + [shift(block, ring, k, size) for k in range(1, size)]


def ring_sum(part, ring, size):
    rows = part.shape[0] // size
    terms = [part[:rows]]
    for k in range(1, size):
        terms.append(shift(part[k * rows : (k + 1) * rows], ring, size - k, size))
    return terms


def add_up(terms):
    total = terms[0].astype(f32)
    for t in terms[1:]:
        total = total + t.astype(f32)
    return total


def pair_sum(total, pair):
    half = total.shape[0] // 2
    return (total[:half] + swap(total[half:].astype(bf16), pair).astype(f32)).astype(bf16)


def spread(block, axes, count):
    return lax.all_to_all(jnp.broadcast_to(block[None], (count,) + block.shape), axes, 0, 0)


def per_device(sizes, query_cache, passage_cache, positive, query_tokens, passage_tokens,
               query_lengths, passage_lengths, norm_gain, adapter_down, adapter_up):
    nx, nyl, nz, nyh, nc = sizes
    n_all = nx * nyl * nz * nyh * nc
    n_pb, n_pa = nx * nyl, nz * nyh * nc
    x_i, yl_i, z_i, yh_i, c_i = (lax.axis_index(a) for a in everyone)
    first_core = c_i == 0
    own_queries, own_passages = query_cache[0], passage_cache[0]
    width = own_queries.shape[1]
    qrow, prow = own_queries.shape[0], own_passages.shape[0]
    d_own, hidden_width = adapter_down.shape
    r_own = adapter_up.shape[0]
    q_seqs, p_seqs = query_lengths.shape[-1], passage_lengths.shape[-1]

    q_pair = jnp.concatenate([own_queries, swap(own_queries, "yh")], axis=0)
    p_pair = jnp.concatenate([own_passages, swap(own_passages, "yl")], axis=0)
    queries = jnp.concatenate(ring_parts(q_pair, "z", nz), axis=0)
    mine_p = jnp.concatenate(ring_parts(p_pair, "x", nx), axis=0)
    other_p = swap(mine_p, "c")
    passages = jnp.concatenate([mine_p, other_p], axis=0)

    gain = norm_gain.astype(f32)
    gained_down = (adapter_down.astype(f32) * gain[:, None]).astype(bf16)
    near = spread(gained_down, ("yl", "z", "yh"), nyl * nz * nyh)
    near_other = swap(near, "c")
    near = jnp.stack(
        [jnp.where(first_core, near, near_other), jnp.where(first_core, near_other, near)], axis=1
    ).reshape(-1, hidden_width)
    half_rows = near.shape[0] // 2
    near_half = lax.dynamic_slice_in_dim(near, c_i * half_rows, half_rows, axis=0)
    far = [shift(near_half, "x", k, nx) for k in range(1, nx)]
    far_other = swap(jnp.stack(far), "c")
    down_full = jnp.zeros((width, hidden_width), bf16)
    down_full = lax.dynamic_update_slice_in_dim(down_full, near, x_i * 2 * half_rows, axis=0)
    for k in range(1, nx):
        base = lax.rem(x_i - k + nx, nx) * 2 * half_rows
        down_full = lax.dynamic_update_slice_in_dim(down_full, far[k - 1], base + c_i * half_rows, axis=0)
        down_full = lax.dynamic_update_slice_in_dim(
            down_full, far_other[k - 1], base + (1 - c_i) * half_rows, axis=0
        )

    up_near = spread(adapter_up, ("x", "yl", "yh"), nx * nyl * nyh).reshape(-1, width)
    up_half = jnp.concatenate(ring_parts(up_near, "z", nz), axis=0)
    up_other = swap(up_half, "c")

    contract = (((1,), (1,)), ((), ()))
    scores = jnp.concatenate(
        [
            lax.dot_general(queries, mine_p, contract, preferred_element_type=f32),
            lax.dot_general(queries, other_p, contract, preferred_element_type=f32),
        ],
        axis=1,
    ) * scale
    local_top = jnp.max(scores, axis=1)
    local_sum = jnp.sum(jnp.exp(scores - local_top[:, None]), axis=1)

    m_i = z_i * nyh + yh_i
    groups = nz * nyh
    step = jnp.arange(groups, dtype=jnp.int32)
    owner = lax.rem(z_i - step // nyh + nz, nz) * nyh + lax.rem(yh_i - step % nyh + nyh, nyh)
    pick = owner[:, None] == step[None, :]

    def to_owner(v):
        return jnp.sum(jnp.where(pick[:, :, None], v.reshape(groups, 1, qrow), 0), axis=0)

    def to_step(v):
        return jnp.sum(jnp.where(pick[:, :, None], v.reshape(1, groups, qrow), 0), axis=1).reshape(-1)

    packet = jnp.concatenate(
        [to_owner(local_top).reshape(-1), to_owner(local_sum).reshape(-1), positive[0].astype(f32)]
    )
    packet = jnp.pad(packet, (0, -packet.shape[0] % 128))
    stats = spread(packet, ("z", "yh"), groups)
    n_q = groups * qrow
    tops, sums = stats[:, :n_q], stats[:, n_q : 2 * n_q]
    row_top = jnp.max(tops, axis=0)
    row_sum = jnp.sum(sums * jnp.exp(tops - row_top[None, :]), axis=0)
    row_top, row_sum = to_step(row_top), to_step(row_sum)
    target = to_step(stats[:, 2 * n_q : 2 * n_q + qrow])

    core_step = jnp.arange(nc, dtype=jnp.int32)[:, None, None, None]
    x_step = jnp.arange(nx, dtype=jnp.int32)[None, :, None, None]
    yl_step = jnp.arange(nyl, dtype=jnp.int32)[None, None, :, None]
    lane = jnp.arange(prow, dtype=jnp.int32)[None, None, None, :]
    a_of = m_i * nc + lax.rem(c_i + core_step, nc)
    b_of = lax.rem(x_i - x_step + nx, nx) * nyl + lax.rem(yl_i - yl_step + nyl, nyl)
    columns = (a_of * (n_pb * prow) + b_of * prow + lane).reshape(-1)

    soft = jnp.exp(scores - row_top[:, None]) / row_sum[:, None]
    hit = (target.astype(jnp.int32)[:, None] == columns[None, :]).astype(f32)
    coupling = barrier((soft - hit).astype(bf16))

    first_q = coupling.reshape(groups, qrow, -1)[:, :q_seqs].reshape(groups * q_seqs, -1)
    q_few = (jnp.dot(first_q, passages, preferred_element_type=f32) * scale).astype(bf16)
    first_p = coupling.reshape(n_q, nc * n_pb, prow)[:, :, :p_seqs].reshape(n_q, nc * n_pb * p_seqs)
    turned = (((0,), (0,)), ((), ()))
    p_few = (lax.dot_general(first_p, queries, turned, preferred_element_type=f32) * scale).astype(bf16)

    def core_sum(part):
        half = part.shape[0] // 2
        return (part[:half].astype(f32) + swap(part[half:], "c").astype(f32)).astype(bf16)

    p_few = core_sum(p_few)
    q_few_terms, p_few_terms = ring_sum(q_few, "z", nz), ring_sum(p_few, "x", nx)

    tokens = jnp.concatenate([query_tokens[0, 0], passage_tokens[0, 0]], axis=0)
    lengths = jnp.concatenate([query_lengths[0, 0], passage_lengths[0, 0]], axis=0)
    n_seq = lengths.shape[0]
    pad = -n_seq % 8
    n_seq8 = n_seq + pad
    rows = tokens.shape[0]
    ends = jnp.cumsum(lengths)
    starts = ends - lengths
    position = jnp.arange(rows, dtype=jnp.int32)[:, None]
    member = (position >= starts[None, :]) & (position < ends[None, :])
    member = jnp.pad(member, ((0, 0), (0, pad))).astype(f32)
    widened = tokens.astype(f32)
    inverse = lax.rsqrt(jnp.mean(widened * widened, axis=1, keepdims=True) + epsilon)
    pre_act = jnp.dot(tokens, down_full, preferred_element_type=f32) * inverse
    active, slope = jax.jvp(lambda v: jax.nn.gelu(v, approximate=True), (pre_act,), (jnp.ones_like(pre_act),))
    active_sums = lax.dot_general(
        member.astype(bf16), active.astype(bf16), turned, preferred_element_type=f32
    ).astype(bf16)
    slope = slope * inverse
    r_block, d_block = hidden_width // n_pb, width // n_pa
    sum_blocks = active_sums.reshape(n_seq8, n_pb, r_block).transpose(1, 0, 2)
    sum_blocks = jnp.pad(sum_blocks, ((0, 0), (0, 0), (0, -r_block % 128)))

    q_few_terms, p_few_terms, slope, sum_blocks = barrier((q_few_terms, p_few_terms, slope, sum_blocks))
    q_few = pair_sum(add_up(q_few_terms), "yh")
    p_few = pair_sum(add_up(p_few_terms), "yl")

    p_part = (
        lax.dot_general(coupling, queries, turned, preferred_element_type=f32) * scale
    ).astype(bf16)
    q_part = (jnp.dot(coupling, passages, preferred_element_type=f32) * scale).astype(bf16)
    q_terms, p_terms = ring_sum(q_part, "z", nz), ring_sum(core_sum(p_part), "x", nx)

    emb_grads = jnp.concatenate([q_few, p_few], axis=0).astype(f32)
    seq_grads = (emb_grads / lengths.astype(f32)[:, None]).astype(bf16)
    seq_grads = jnp.pad(seq_grads, ((0, pad), (0, 0)))

    grad_blocks = seq_grads.reshape(n_seq8, n_pa, d_block).transpose(1, 0, 2)
    packet = jnp.concatenate(
        [
            jnp.broadcast_to(grad_blocks[None], (n_pb,) + grad_blocks.shape),
            jnp.broadcast_to(sum_blocks[:, None], (n_pb, n_pa) + sum_blocks.shape[1:]),
        ],
        axis=-1,
    ).reshape(n_all, n_seq8, -1)
    everything = lax.all_to_all(packet, everyone, 0, 0).reshape(n_all * n_seq8, -1)

    h_rel = jnp.concatenate(
        [
            lax.dot_general(seq_grads, up_half, contract, preferred_element_type=f32),
            lax.dot_general(seq_grads, up_other, contract, preferred_element_type=f32),
        ],
        axis=1,
    )
    here = jnp.arange(hidden_width, dtype=jnp.int32)
    unit, rest = here % r_own, here // r_own
    yh_s, rest = rest % nyh, rest // nyh
    yl_s, rest = rest % nyl, rest // nyl
    x_s, rest = rest % nx, rest // nx
    z_s, c_s = rest % nz, rest // nz
    z_s, c_s = lax.rem(z_i - z_s + nz, nz), lax.rem(c_i + c_s, nc)
    place = ((((x_s * nyl + yl_s) * nz + z_s) * nyh + yh_s) * nc + c_s) * r_own + unit
    order = (place[:, None] == here[None, :]).astype(f32)
    hidden = jnp.dot(h_rel, order, precision=lax.Precision.HIGHEST)
    hidden_rows = jnp.dot(member, hidden, precision=lax.Precision.HIGHEST)
    inner = (slope * hidden_rows).astype(bf16)
    down_part = lax.dot_general(tokens, inner, turned, preferred_element_type=f32).astype(bf16)

    by_core = down_part.reshape(n_all // nc, nc, d_own, -1)
    keep = jnp.where(first_core, by_core[:, 0], by_core[:, 1])
    give = jnp.where(first_core, by_core[:, 1], by_core[:, 0])
    chip_sum = (keep.astype(f32) + swap(give, "c").astype(f32)).astype(bf16)
    arrived = lax.all_to_all(chip_sum, ("x", "yl", "z", "yh"), 0, 0)

    up_block = lax.dot_general(
        everything[:, d_block : d_block + r_block], everything[:, :d_block], turned, preferred_element_type=f32
    ).reshape(nz, nyh, nc, r_own, 1, d_block)

    def trade(block, axis, index):
        first = index == 0
        mine = jnp.where(first, block[..., 0, :, :, :], block[..., 1, :, :, :])
        theirs = swap(jnp.where(first, block[..., 1, :, :, :], block[..., 0, :, :, :]), axis)
        return jnp.concatenate(
            [jnp.where(first, mine, theirs), jnp.where(first, theirs, mine)], axis=-2
        )

    up_block = trade(trade(up_block, "c", c_i), "yh", yh_i)
    z_blocks = [lax.dynamic_index_in_dim(up_block, lax.rem(z_i + k, nz), 0, keepdims=False) for k in range(nz)]
    z_blocks = [z_blocks[0]] + [shift(z_blocks[k], "z", k, nz) for k in range(1, nz)]
    up_grad = jnp.zeros((r_own, nz) + up_block.shape[2:], f32)
    for k in range(nz):
        up_grad = lax.dynamic_update_slice_in_dim(
            up_grad, z_blocks[k][:, None], lax.rem(z_i - k + nz, nz), axis=1
        )
    up_grad = up_grad.reshape(r_own, width)

    query_grad = pair_sum(add_up(q_terms), "yh")
    passage_grad = pair_sum(add_up(p_terms), "yl")

    ungained = jnp.sum(arrived.astype(f32), axis=0)
    down_grad = ungained * gain[:, None]
    gain_grad = jnp.sum(ungained * adapter_down.astype(f32), axis=1)
    return (query_grad[None], passage_grad[None], down_grad, up_grad, gain_grad)


def solution(mesh):
    nyl, nyh, nc = 2, 2, 2
    nx, nz = mesh.shape["pb"] // nyl, mesh.shape["pa"] // (nyh * nc)
    sizes = (nx, nyl, nz, nyh, nc)
    fine = Mesh(mesh.devices.reshape(sizes), everyone)
    pb, pa = ("x", "yl"), ("z", "yh", "c")
    in_specs = (
        P(pb, pa, None),
        P(pa, pb, None),
        P(pb, pa),
        P(pb, pa, None, None),
        P(pa, pb, None, None),
        P(pb, pa, None),
        P(pa, pb, None),
        P(everyone),
        P(everyone, None),
        P(everyone, None),
    )
    out_specs = (P(pb, pa, None), P(pa, pb, None), P(everyone, None), P(everyone, None), P(everyone))

    def body(*args):
        return per_device(sizes, *args)

    return jax.shard_map(body, mesh=fine, in_specs=in_specs, out_specs=out_specs, check_vma=False)
```

```python
import jax
import jax.numpy as jnp
from jax import lax
from jax.experimental import pallas as pl
from jax.experimental.pallas import tpu as pltpu
from jax.sharding import Mesh, PartitionSpec as P

scale = 1.0 / 0.05
epsilon = 1e-06
bf16 = jnp.bfloat16
f32 = jnp.float32
everyone = ("x", "yl", "z", "yh", "c")
swap2 = [(0, 1), (1, 0)]
barrier = lax.optimization_barrier


def shift(value, axis, step, size):
    return lax.ppermute(value, axis, [(i, (i + step) % size) for i in range(size)])


def swap(value, axis):
    return lax.ppermute(value, axis, swap2)


def ring_sides(block, ring):
    return shift(block, ring, 1, 4), shift(block, ring, 3, 4)


def ring_far(before, after, ring):
    half = before.shape[0] // 2
    return shift(before[:half], ring, 1, 4), shift(after[half:], ring, 3, 4)


def ring_sum(parts, ring, size):
    return [parts[0]] + [shift(parts[k], ring, size - k, size) for k in range(1, size)]


def cut_rows(part, count):
    rows = part.shape[0] // count
    return [part[k * rows : (k + 1) * rows] for k in range(count)]


def add_up(terms):
    total = terms[0].astype(f32)
    for t in terms[1:]:
        total = total + t.astype(f32)
    return total


def pair_sum(total, pair):
    half = total.shape[0] // 2
    return (total[:half] + swap(total[half:].astype(bf16), pair).astype(f32)).astype(bf16)


gelu_root = 0.7978845608028654
gelu_cube = 0.044715
kernel_room = pltpu.CompilerParams(vmem_limit_bytes=60 * 1024 * 1024)
light = pl.CostEstimate(flops=0, bytes_accessed=0, transcendentals=0)
any_space = pl.BlockSpec(memory_space=pl.ANY)
in_vmem = pl.BlockSpec(memory_space=pltpu.VMEM)
in_smem = pl.BlockSpec(memory_space=pltpu.SMEM)


turned = (((0,), (0,)), ((), ()))
contract = (((1,), (1,)), ((), ()))


def load_blocks(parts, wholes, sems):
    copies, n = [], 0
    for blocks, whole in zip(parts, wholes):
        row = 0
        for block in blocks:
            copies.append(pltpu.make_async_copy(block, whole.at[pl.ds(row, block.shape[0])], sems.at[n]))
            row, n = row + block.shape[0], n + 1
    for c in copies:
        c.start()
    return copies


def wait_all(copies):
    for c in copies:
        c.wait()


def score_kernel(n_q, n_p, *refs):
    q_blocks, p_blocks = refs[:n_q], refs[n_q : n_q + n_p]
    scores, top, total, q_all, p_all, sems = refs[n_q + n_p :]
    wait_all(load_blocks((q_blocks, p_blocks), (q_all, p_all), sems))
    s = lax.dot_general(q_all[...], p_all[...], contract, preferred_element_type=f32) * scale
    scores[...] = s
    m = jnp.max(s, axis=1, keepdims=True)
    top[...] = m
    total[...] = jnp.sum(jnp.exp(s - m), axis=1, keepdims=True)


def rows_of(blocks):
    return sum(b.shape[0] for b in blocks)


def block_scratch(q_blocks, p_blocks):
    width = q_blocks[0].shape[1]
    return [
        pltpu.VMEM((rows_of(q_blocks), width), bf16),
        pltpu.VMEM((rows_of(p_blocks), width), bf16),
        pltpu.SemaphoreType.DMA((len(q_blocks) + len(p_blocks),)),
    ]


def score_block(q_blocks, p_blocks):
    n_q, n_p = rows_of(q_blocks), rows_of(p_blocks)
    column = jax.ShapeDtypeStruct((n_q, 1), f32)
    return pl.pallas_call(
        lambda *refs: score_kernel(len(q_blocks), len(p_blocks), *refs),
        out_shape=(jax.ShapeDtypeStruct((n_q, n_p), f32), column, column),
        in_specs=[any_space] * (len(q_blocks) + len(p_blocks)),
        out_specs=(in_vmem,) * 3,
        scratch_shapes=block_scratch(q_blocks, p_blocks),
        compiler_params=kernel_room,
        cost_estimate=light,
    )(*q_blocks, *p_blocks)


def couple_kernel(n_q, n_p, sizes, counts, spot, scores, stat, columns, *refs):
    q_blocks, p_blocks = refs[:n_q], refs[n_q : n_q + n_p]
    coupling, q_few, p_few, q_all, p_all, sems = refs[n_q + n_p :]
    copies = load_blocks((q_blocks, p_blocks), (q_all, p_all), sems)
    soft = jnp.exp(scores[...] - stat[:, 0:1]) / stat[:, 1:2]
    hit = (stat[:, 2:3].astype(jnp.int32) == columns[...]).astype(f32)
    link = (soft - hit).astype(bf16)
    coupling[...] = link
    wait_all(copies)
    rows, cols = link.shape
    nx, nyl, nz, nyh, nc = sizes
    yl, yh, core, x, z = (spot[k] for k in range(head))
    q_seqs, q_row, p_seqs, p_row = counts
    n_q_owners = q_few.shape[0]

    n_few = n_q_owners * q_seqs
    few_i = lax.broadcasted_iota(jnp.int32, (n_few, rows), 0)
    here = lax.broadcasted_iota(jnp.int32, (n_few, rows), 1)
    seq, owner = few_i % q_seqs, few_i // q_seqs
    step = (z - owner // nyh + nz) % nz * nyh + (yh - owner % nyh + nyh) % nyh
    pick = (here == step * q_row + seq).astype(bf16)
    first = jnp.dot(pick, link, preferred_element_type=f32).astype(bf16)
    found = jnp.dot(first, p_all[...], preferred_element_type=f32) * scale
    for k in range(n_q_owners):
        q_few[k] = found[k * q_seqs : (k + 1) * q_seqs].astype(bf16)

    n_few = p_few.shape[0] * p_seqs
    few_i = lax.broadcasted_iota(jnp.int32, (n_few, cols), 0)
    here = lax.broadcasted_iota(jnp.int32, (n_few, cols), 1)
    seq, owner = few_i % p_seqs, few_i // p_seqs
    x_step = (x - owner // (nyl * nc) + nx) % nx
    yl_step = (yl - owner // nc % nyl + nyl) % nyl
    core_step = (core - owner % nc + nc) % nc
    pick = (here == ((core_step * nx + x_step) * nyl + yl_step) * p_row + seq).astype(bf16)
    first = lax.dot_general(pick, link, contract, preferred_element_type=f32).astype(bf16)
    found = jnp.dot(first, q_all[...], preferred_element_type=f32) * scale
    for k in range(p_few.shape[0]):
        p_few[k] = found[k * p_seqs : (k + 1) * p_seqs].astype(bf16)


def couple(spot, scores, stat, columns, q_blocks, p_blocks, sizes, counts):
    n_q, n_p = scores.shape
    width = q_blocks[0].shape[1]
    q_seqs, q_row, p_seqs, p_row = counts
    return pl.pallas_call(
        lambda *refs: couple_kernel(len(q_blocks), len(p_blocks), sizes, counts, *refs),
        out_shape=(
            jax.ShapeDtypeStruct((n_q, n_p), bf16),
            jax.ShapeDtypeStruct((n_q // q_row, q_seqs, width), bf16),
            jax.ShapeDtypeStruct((n_p // p_row, p_seqs, width), bf16),
        ),
        in_specs=[in_smem] + [in_vmem] * 3 + [any_space] * (len(q_blocks) + len(p_blocks)),
        out_specs=[in_vmem] * 3,
        scratch_shapes=block_scratch(q_blocks, p_blocks),
        compiler_params=kernel_room,
        cost_estimate=light,
    )(spot, scores, stat, columns, *q_blocks, *p_blocks)


def ring_add_kernel(n, *refs):
    total = refs[0][...].astype(f32)
    for r in refs[1:n]:
        total = total + r[...].astype(f32)
    half = total.shape[0] // 2
    refs[n][...] = total[:half]
    refs[n + 1][...] = total[half:].astype(bf16)


def ring_add(terms):
    rows, width = terms[0].shape
    tile = width // 4

    def cut(n):
        return pl.BlockSpec((n, tile), lambda i: (0, i))

    return pl.pallas_call(
        lambda *refs: ring_add_kernel(len(terms), *refs),
        grid=(4,),
        out_shape=(jax.ShapeDtypeStruct((rows // 2, width), f32), jax.ShapeDtypeStruct((rows // 2, width), bf16)),
        in_specs=[cut(rows)] * len(terms),
        out_specs=(cut(rows // 2),) * 2,
        compiler_params=kernel_room,
        cost_estimate=pl.CostEstimate(
            flops=0, bytes_accessed=2 * rows * width * (len(terms) + 2), transcendentals=0
        ),
    )(*terms)


def core_add_kernel(n, *refs):
    for keep, came, out in zip(refs[:n], refs[n : 2 * n], refs[2 * n :]):
        out[...] = (keep[...].astype(f32) + came[...].astype(f32)).astype(bf16)


def core_add(keep, came):
    steps = 4
    width = keep[0].shape[-1]

    def cut(a):
        return pl.BlockSpec(a.shape[:-1] + (width // steps,), lambda i: (0,) * (a.ndim - 1) + (i,))

    return pl.pallas_call(
        lambda *refs: core_add_kernel(len(keep), *refs),
        grid=(steps,),
        out_shape=[jax.ShapeDtypeStruct(a.shape, bf16) for a in keep],
        in_specs=[cut(a) for a in (*keep, *came)],
        out_specs=[cut(a) for a in keep],
        compiler_params=kernel_room,
        cost_estimate=light,
    )(*keep, *came)


def chip_add_kernel(n, keep, *refs):
    out = refs[n]
    rows = refs[0].shape[0]
    for k in range(n):
        here = pl.ds(k * rows, rows)
        out[here] = (keep[here].astype(f32) + refs[k][...].astype(f32)).astype(bf16)


def chip_add(keep, came):
    steps = 4
    width = keep.shape[-1]

    def cut(a):
        return pl.BlockSpec(a.shape[:-1] + (width // steps,), lambda i: (0,) * (a.ndim - 1) + (i,))

    return pl.pallas_call(
        lambda *refs: chip_add_kernel(len(came), *refs),
        grid=(steps,),
        out_shape=jax.ShapeDtypeStruct(keep.shape, bf16),
        in_specs=[cut(keep)] + [cut(a) for a in came],
        out_specs=cut(keep),
        compiler_params=kernel_room,
        cost_estimate=light,
    )(keep, *came)


def parts_kernel(n_blocks, n_out, turn, coupling, *refs):
    blocks, outs = refs[:n_blocks], refs[n_blocks : n_blocks + n_out]
    link = coupling[...]
    rows = outs[0].shape[0]
    whole = jnp.concatenate([b[...] for b in blocks], axis=0)
    if turn:
        part = lax.dot_general(link, whole, turned, preferred_element_type=f32)
    else:
        part = jnp.dot(link, whole, preferred_element_type=f32)
    part = (part * scale).astype(bf16)
    for k in range(n_out):
        outs[k][...] = part[k * rows : (k + 1) * rows]


def grad_parts(coupling, blocks, n_out, turn):
    n_q, n_p = coupling.shape
    width = blocks[0].shape[1]
    tile = 512
    rows = (n_p if turn else n_q) // n_out

    def cut(n):
        return pl.BlockSpec((n, tile), lambda i: (0, i))

    return pl.pallas_call(
        lambda *refs: parts_kernel(len(blocks), n_out, turn, *refs),
        grid=(width // tile,),
        out_shape=[jax.ShapeDtypeStruct((rows, width), bf16)] * n_out,
        in_specs=[pl.BlockSpec((n_q, n_p), lambda i: (0, 0))] + [cut(b.shape[0]) for b in blocks],
        out_specs=[cut(rows)] * n_out,
        compiler_params=kernel_room,
        cost_estimate=pl.CostEstimate(
            flops=2 * n_q * n_p * width, bytes_accessed=2 * (n_q + n_p) * width, transcendentals=0
        ),
    )(coupling, *blocks)


def down_kernel(core, tok_q, tok_p, inner_q, inner_p, keep, *gives):
    part = lax.dot_general(tok_p[...], inner_p[...], turned, preferred_element_type=f32)
    part = part + lax.dot_general(tok_q[...], inner_q[...], turned, preferred_element_type=f32)
    chips, rows, hidden = keep.shape
    part = part.astype(bf16).reshape(chips, 2, rows, hidden)
    first = core[2] == 0
    piece = pl.program_id(0) // (pl.num_programs(0) // len(gives))

    @pl.when(first)
    def _():
        keep[...] = part[:, 0]

    @pl.when(jnp.logical_not(first))
    def _():
        keep[...] = part[:, 1]

    for k, give in enumerate(gives):

        @pl.when((piece == k) & first)
        def _():
            give[...] = part[:, 1]

        @pl.when((piece == k) & jnp.logical_not(first))
        def _():
            give[...] = part[:, 0]


def down_parts(spot, tok_q, tok_p, inner_q, inner_p, rows):
    width, hidden = tok_q.shape[1], inner_q.shape[1]
    tile, pieces = 512, 4
    chips = tile // (2 * rows)
    steps = width // tile
    each = steps // pieces
    n_chips = width // (2 * rows)

    def cut(a):
        return pl.BlockSpec((a.shape[0], tile), lambda i: (0, i))

    def piece_spec(k):
        return pl.BlockSpec((chips, rows, hidden), lambda i: (jnp.clip(i - k * each, 0, each - 1), 0, 0))

    out = pl.pallas_call(
        down_kernel,
        grid=(steps,),
        out_shape=[jax.ShapeDtypeStruct((n_chips, rows, hidden), bf16)]
        + [jax.ShapeDtypeStruct((n_chips // pieces, rows, hidden), bf16)] * pieces,
        in_specs=[
            in_smem, cut(tok_q), cut(tok_p),
            pl.BlockSpec(inner_q.shape, lambda i: (0, 0)), pl.BlockSpec(inner_p.shape, lambda i: (0, 0)),
        ],
        out_specs=[pl.BlockSpec((chips, rows, hidden), lambda i: (i, 0, 0))] + [piece_spec(k) for k in range(pieces)],
        compiler_params=kernel_room,
        cost_estimate=pl.CostEstimate(
            flops=2 * (tok_q.shape[0] + tok_p.shape[0]) * width * hidden, bytes_accessed=4 * width * hidden,
            transcendentals=0,
        ),
    )(spot, tok_q, tok_p, inner_q, inner_p)
    return out[0], out[1:]


ring_places = ((0, 0, 2), (1, 0, 2), (2, 0, 1), (2, 1, 1), (3, 0, 2))
head = 5


def token_kernel(n_seq, n_blocks, spot, *rest):
    blocks = rest[:n_blocks]
    tok_q, tok_p, slope_q, slope_p, sums, weights, sems = rest[n_blocks:]
    i = pl.program_id(0)

    @pl.when(i == 0)
    def _():
        copies = []
        for k in range(n_blocks):
            step, first, count = ring_places[k % len(ring_places)]
            x = lax.rem(spot[3] - step + 4, 4)
            core = lax.rem(spot[2] + k // len(ring_places), 2)
            copies.append(
                pltpu.make_async_copy(
                    blocks[k].at[:, :, :, pl.ds(0, weights.shape[5])],
                    weights.at[x, pl.ds(first, count), :, :, core],
                    sems.at[k],
                )
            )
        for c in copies:
            c.start()
        sums[...] = jnp.zeros_like(sums)
        for c in copies:
            c.wait()

    hidden = weights.shape[-1]

    def work(tok, slope, first_row):
        rows = tok.shape[0]
        wide = tok[...].astype(f32)
        inverse = lax.rsqrt(jnp.mean(wide * wide, axis=1, keepdims=True) + epsilon)
        pre = jnp.dot(tok[...], weights[...].reshape(-1, hidden), preferred_element_type=f32) * inverse
        square = pre * pre
        bend = jnp.tanh(gelu_root * pre * (1.0 + gelu_cube * square))
        up = 0.5 * (1.0 + bend)
        active = (pre * up).astype(bf16)
        steep = up + 0.5 * pre * (1.0 - bend * bend) * (gelu_root * (1.0 + 3.0 * gelu_cube * square))
        slope[...] = steep * inverse
        seq = lax.broadcasted_iota(jnp.int32, (sums.shape[0], rows), 0)
        row = lax.broadcasted_iota(jnp.int32, (sums.shape[0], rows), 1) + first_row
        member = jnp.zeros((sums.shape[0], rows), f32)
        for k in range(n_seq):
            inside = (row >= spot[head + k]) & (row < spot[head + n_seq + k]) & (seq == k)
            member = jnp.where(inside, 1.0, member)
        sums[...] += jnp.dot(member.astype(bf16), active, preferred_element_type=f32)

    @pl.when(i == 0)
    def _():
        work(tok_q, slope_q, 0)

    @pl.when(i > 0)
    def _():
        work(tok_p, slope_p, tok_q.shape[0] + (i - 1) * tok_p.shape[0])


def token_half(spot, blocks, tok_q, tok_p, n_seq, n_seq8):
    width = tok_q.shape[1]
    nyl, nz, nyh, both, hidden = blocks[0].shape
    d_own = width // (4 * nyl * nz * nyh * 2)
    steps = 3
    tile = tok_p.shape[0] // steps

    def tile_of(i):
        return (jnp.maximum(i - 1, 0), 0)

    return pl.pallas_call(
        lambda *refs: token_kernel(n_seq, len(blocks), *refs),
        grid=(steps + 1,),
        out_shape=(
            jax.ShapeDtypeStruct((tok_q.shape[0], hidden), f32),
            jax.ShapeDtypeStruct((tok_p.shape[0], hidden), f32),
            jax.ShapeDtypeStruct((n_seq8, hidden), f32),
        ),
        in_specs=[in_smem] + [any_space] * len(blocks)
        + [pl.BlockSpec(tok_q.shape, lambda i: (0, 0)), pl.BlockSpec((tile, width), tile_of)],
        out_specs=(
            pl.BlockSpec((tok_q.shape[0], hidden), lambda i: (0, 0)),
            pl.BlockSpec((tile, hidden), tile_of),
            pl.BlockSpec((n_seq8, hidden), lambda i: (0, 0)),
        ),
        scratch_shapes=[
            pltpu.VMEM((4, nyl, nz, nyh, 2, d_own, hidden), bf16), pltpu.SemaphoreType.DMA((len(blocks),))
        ],
        compiler_params=kernel_room,
        cost_estimate=light,
    )(spot, *blocks, tok_q, tok_p)


def hidden_kernel(n_blocks, units, grads, *refs):
    blocks = refs[:n_blocks]
    out, lines, sems = refs[n_blocks:]
    rows, line = lines.shape[-2:]
    copies = [
        pltpu.make_async_copy(
            blocks[k].at[:, :, :, pl.ds(blocks[k].shape[3] - rows, rows)],
            lines.at[step, pl.ds(first, count)],
            sems.at[k],
        )
        for k, (step, first, count) in enumerate(ring_places)
    ]
    for c in copies:
        c.start()
    n_seq, width = grads.shape
    per_unit = width // line
    cut = jnp.concatenate([grads[:, j * line : (j + 1) * line] for j in range(per_unit)], axis=0)
    for c in copies:
        c.wait()
    flat = lines[...].reshape(-1, line)
    found = lax.dot_general(cut, flat, contract, preferred_element_type=f32)
    which = lax.broadcasted_iota(jnp.int32, (n_seq, flat.shape[0]), 1) % per_unit
    kept = jnp.zeros((n_seq, flat.shape[0]), f32)
    for j in range(per_unit):
        kept = jnp.where(which == j, found[j * n_seq : (j + 1) * n_seq], kept)
    source = lax.broadcasted_iota(jnp.int32, (flat.shape[0], units), 0) // per_unit
    to = lax.broadcasted_iota(jnp.int32, (flat.shape[0], units), 1)
    gather = (source == to).astype(bf16)
    total = jnp.zeros((n_seq, units), f32)
    for _ in range(3):
        piece = kept.astype(bf16)
        total = total + jnp.dot(piece, gather, preferred_element_type=f32)
        kept = kept - piece.astype(f32)
    out[...] = total


def hidden_of(grads, blocks, rows, units):
    shape = blocks[0].shape
    return pl.pallas_call(
        lambda *refs: hidden_kernel(len(blocks), units, *refs),
        out_shape=jax.ShapeDtypeStruct((grads.shape[0], units), f32),
        in_specs=[in_vmem] + [any_space] * len(blocks),
        out_specs=in_vmem,
        scratch_shapes=[
            pltpu.VMEM((4,) + shape[:3] + (rows, shape[4]), bf16), pltpu.SemaphoreType.DMA((len(blocks),))
        ],
        compiler_params=kernel_room,
        cost_estimate=light,
    )(grads, *blocks)


def inner_kernel(n_seq, spot, own, other, order, slope_q, slope_p, inner_q, inner_p):
    found = jnp.concatenate([own[...], other[...]], axis=1)
    hidden = jnp.zeros_like(found)
    for _ in range(3):
        piece = found.astype(bf16)
        hidden = hidden + jnp.dot(piece, order[...], preferred_element_type=f32)
        found = found - piece.astype(f32)
    first_row = 0
    for slope, inner in ((slope_q, inner_q), (slope_p, inner_p)):
        row = lax.broadcasted_iota(jnp.int32, (slope.shape[0], 1), 0) + first_row
        spread_out = jnp.zeros(slope.shape, f32)
        for k in range(n_seq):
            inside = (row >= spot[head + k]) & (row < spot[head + n_seq + k])
            spread_out = jnp.where(inside, hidden[k : k + 1, :], spread_out)
        inner[...] = (slope[...] * spread_out).astype(bf16)
        first_row += slope.shape[0]


def inner_of(spot, own, other, order, slope_q, slope_p, n_seq):
    return pl.pallas_call(
        lambda *refs: inner_kernel(n_seq, *refs),
        out_shape=(jax.ShapeDtypeStruct(slope_q.shape, bf16), jax.ShapeDtypeStruct(slope_p.shape, bf16)),
        in_specs=[in_smem] + [in_vmem] * 5,
        out_specs=(in_vmem,) * 2,
        compiler_params=kernel_room,
        cost_estimate=light,
    )(spot, own, other, order, slope_q, slope_p)


def spread(block, axes, count):
    return lax.all_to_all(jnp.broadcast_to(block[None], (count,) + block.shape), axes, 0, 0)


def per_device(sizes, query_cache, passage_cache, positive, query_tokens, passage_tokens,
               query_lengths, passage_lengths, norm_gain, adapter_down, adapter_up):
    nx, nyl, nz, nyh, nc = sizes
    n_all = nx * nyl * nz * nyh * nc
    n_pb, n_pa = nx * nyl, nz * nyh * nc
    x_i, yl_i, z_i, yh_i, c_i = (lax.axis_index(a) for a in everyone)
    first_core = c_i == 0
    own_queries, own_passages = query_cache[0], passage_cache[0]
    width = own_queries.shape[1]
    qrow, prow = own_queries.shape[0], own_passages.shape[0]
    d_own, hidden_width = adapter_down.shape
    r_own = adapter_up.shape[0]
    q_seqs, p_seqs = query_lengths.shape[-1], passage_lengths.shape[-1]

    chips = ("x", "yl", "z", "yh")
    n_chips = n_all // nc
    gain = norm_gain.astype(f32)
    gained_down = (adapter_down.astype(f32) * gain[:, None]).astype(bf16)
    (q_next, p_next, gained_down, adapter_up, query_lengths, passage_lengths, yl_i, yh_i, c_i) = barrier(
        (swap(own_queries, "yh"), swap(own_passages, "yl"), gained_down, adapter_up,
         query_lengths, passage_lengths, yl_i, yh_i, c_i)
    )

    q_pair = jnp.concatenate([own_queries, q_next], axis=0)
    p_pair = jnp.concatenate([own_passages, p_next], axis=0)
    q_before, q_after = ring_sides(q_pair, "z")
    p_before, p_after = ring_sides(p_pair, "x")
    q_blocks = [q_pair, q_before, *ring_far(q_before, q_after, "z"), q_after]
    p_blocks = [p_pair, p_before, *ring_far(p_before, p_after, "x"), p_after]
    p_other = swap(p_pair, "c")

    tok_q, tok_p = query_tokens[0, 0], passage_tokens[0, 0]
    lengths = jnp.concatenate([query_lengths[0, 0], passage_lengths[0, 0]], axis=0)
    n_seq = lengths.shape[0]
    pad = -n_seq % 8
    n_seq8 = n_seq + pad
    ends = jnp.cumsum(lengths)
    spot = jnp.concatenate([jnp.stack([yl_i, yh_i, c_i, x_i, z_i]), ends - lengths, ends]).astype(jnp.int32)

    here = jnp.arange(hidden_width, dtype=jnp.int32)
    unit, rest = here % r_own, here // r_own
    yh_s, rest = rest % nyh, rest // nyh
    z_s, rest = rest % nz, rest // nz
    yl_s, rest = rest % nyl, rest // nyl
    x_s, c_s = lax.rem(x_i - rest % nx + nx, nx), lax.rem(c_i + rest // nx, nc)
    place = ((((x_s * nyl + yl_s) * nz + z_s) * nyh + yh_s) * nc + c_s) * r_own + unit
    order = (place[:, None] == here[None, :]).astype(bf16)

    q_blocks, p_blocks, p_other, spot, order, gained_down, adapter_up = barrier(
        (q_blocks, p_blocks, p_other, spot, order, gained_down, adapter_up)
    )
    near = spread(
        jnp.concatenate([gained_down, adapter_up.reshape(-1, hidden_width)], axis=0),
        ("yl", "z", "yh"), nyl * nz * nyh,
    ).reshape(nyl, nz, nyh, -1, hidden_width)
    p_blocks = barrier(p_blocks + [p_other] + [swap(b, "c") for b in p_blocks[1:]])

    scores, local_top, local_sum = score_block(q_blocks, p_blocks)

    m_i = z_i * nyh + yh_i
    groups = nz * nyh
    step = jnp.arange(groups, dtype=jnp.int32)
    owner = lax.rem(z_i - step // nyh + nz, nz) * nyh + lax.rem(yh_i - step % nyh + nyh, nyh)
    pick = owner[:, None] == step[None, :]

    def to_owner(v):
        return jnp.sum(jnp.where(pick[:, :, None], v.reshape(groups, 1, qrow), 0), axis=0)

    def to_step(v):
        return jnp.sum(jnp.where(pick[:, :, None], v.reshape(1, groups, qrow), 0), axis=1).reshape(-1)

    packet = jnp.concatenate(
        [to_owner(local_top).reshape(-1), to_owner(local_sum).reshape(-1), positive[0].astype(f32)]
    )
    packet = jnp.pad(packet, (0, -packet.shape[0] % 128))
    packet, near = barrier((packet, near))
    near_down, near_up = near[:, :, :, :d_own], near[:, :, :, d_own:]
    down_before, down_after = ring_sides(near_down, "x")
    up_before, up_after = ring_sides(near_up, "x")
    stats = spread(packet, ("z", "yh"), groups)

    stats, down_before, down_after = barrier((stats, down_before, down_after))
    down_far = ring_far(down_before, down_after, "x")
    n_q = groups * qrow
    tops, sums = stats[:, :n_q], stats[:, n_q : 2 * n_q]
    row_top = jnp.max(tops, axis=0)
    row_sum = jnp.sum(sums * jnp.exp(tops - row_top[None, :]), axis=0)
    target = stats[:, 2 * n_q : 2 * n_q + qrow]
    stat = jnp.stack([to_step(row_top), to_step(row_sum), to_step(target)], axis=1)

    core_step = jnp.arange(nc, dtype=jnp.int32)[:, None, None, None]
    x_step = jnp.arange(nx, dtype=jnp.int32)[None, :, None, None]
    yl_step = jnp.arange(nyl, dtype=jnp.int32)[None, None, :, None]
    lane = jnp.arange(prow, dtype=jnp.int32)[None, None, None, :]
    a_of = m_i * nc + lax.rem(c_i + core_step, nc)
    b_of = lax.rem(x_i - x_step + nx, nx) * nyl + lax.rem(yl_i - yl_step + nyl, nyl)
    columns = (a_of * (n_pb * prow) + b_of * prow + lane).reshape(-1)

    coupling, q_few, p_few = couple(
        spot, scores, stat, columns[None, :], q_blocks, p_blocks, sizes, (q_seqs, qrow, p_seqs, prow)
    )
    p_few = lax.all_to_all(p_few, ("x", "yl", "c"), 0, 0)
    q_few = lax.all_to_all(q_few, ("z", "yh"), 0, 0)

    q_part = grad_parts(coupling, p_blocks, nz, False)
    coupling, q_few, q_part, up_before, up_after = barrier((coupling, q_few, q_part, up_before, up_after))
    up_far = ring_far(up_before, up_after, "x")
    p_part = grad_parts(coupling, q_blocks, nc * nx, True)
    p_keep, p_give = p_part[:nx], p_part[nx:]

    p_few, p_keep, p_give, down_far, up_far, q_terms = barrier(
        (p_few, p_keep, p_give, down_far, up_far, ring_sum(q_part, "z", nz))
    )
    down_x = [near_down, down_before, *down_far, down_after]
    up_x = [near_up, up_before, *up_far, up_after]

    p_sum = core_add(p_keep, [swap(b, "c") for b in p_give])
    down_blocks, p_sum = barrier((down_x + [swap(b, "c") for b in down_x], p_sum))
    slope_q, slope_p, active_sums = token_half(spot, down_blocks, tok_q, tok_p, n_seq, n_seq8)
    r_block, d_block = hidden_width // n_pb, width // n_pa
    sum_blocks = active_sums.astype(bf16).reshape(n_seq8, n_pb, r_block).transpose(1, 0, 2)
    sum_blocks = jnp.pad(sum_blocks, ((0, 0), (0, 0), (0, -r_block % 128)))
    q_few = jnp.sum(q_few.astype(f32), axis=0).astype(bf16)
    p_few = jnp.sum(p_few.astype(f32), axis=0).astype(bf16)

    emb_grads = jnp.concatenate([q_few, p_few], axis=0).astype(f32)
    seq_grads = (emb_grads / lengths.astype(f32)[:, None]).astype(bf16)
    seq_grads = jnp.pad(seq_grads, ((0, pad), (0, 0)))

    grad_blocks = seq_grads.reshape(n_seq8, n_pa, d_block).transpose(1, 0, 2)
    packet = jnp.concatenate(
        [
            jnp.broadcast_to(grad_blocks[None], (n_pb,) + grad_blocks.shape),
            jnp.broadcast_to(sum_blocks[:, None], (n_pb, n_pa) + sum_blocks.shape[1:]),
        ],
        axis=-1,
    ).reshape(n_all, n_seq8, -1)

    seq_both = jnp.concatenate([seq_grads, swap(seq_grads, "c")], axis=0)
    p_terms = ring_sum(p_sum, "x", nx)

    hidden = hidden_of(seq_both, up_x, r_own * width // hidden_width, hidden_width // nc)
    inner_q, inner_p = inner_of(
        spot, hidden[:n_seq8], swap(hidden[n_seq8:], "c"), order, slope_q, slope_p, n_seq
    )
    inner_q, inner_p, p_terms, packet = barrier((inner_q, inner_p, p_terms, packet))
    everything = lax.all_to_all(packet, everyone, 0, 0).reshape(n_all * n_seq8, -1)
    q_own, q_away = ring_add(q_terms)
    p_own, p_away = ring_add(p_terms)
    keep, give = down_parts(spot, tok_q, tok_p, inner_q, inner_p, d_own)
    keep, give, q_own, q_away, p_own, p_away, everything = barrier(
        (keep, give, q_own, q_away, p_own, p_away, everything)
    )
    chip_sum = chip_add(keep, [swap(b, "c") for b in give])
    up_block = lax.dot_general(
        everything[:, d_block : d_block + r_block], everything[:, :d_block], turned, preferred_element_type=f32
    ).reshape(nz, nyh, nc, r_own, 1, d_block)

    def trade(block, axis, index):
        first = index == 0
        mine = jnp.where(first, block[..., 0, :, :, :], block[..., 1, :, :, :])
        theirs = swap(jnp.where(first, block[..., 1, :, :, :], block[..., 0, :, :, :]), axis)
        return jnp.concatenate(
            [jnp.where(first, mine, theirs), jnp.where(first, theirs, mine)], axis=-2
        )

    up_block = trade(trade(up_block, "c", c_i), "yh", yh_i)
    z_blocks = [lax.dynamic_index_in_dim(up_block, lax.rem(z_i + k, nz), 0, keepdims=False) for k in range(nz)]
    z_blocks = [z_blocks[0]] + [shift(z_blocks[k], "z", k, nz) for k in range(1, nz)]
    chip_sum, z_blocks = barrier((chip_sum, z_blocks))
    query_grad = (q_own + swap(q_away, "yh").astype(f32)).astype(bf16)
    passage_grad = (p_own + swap(p_away, "yl").astype(f32)).astype(bf16)
    arrived = lax.all_to_all(chip_sum, chips, 0, 0)

    up_grad = jnp.zeros((r_own, nz) + up_block.shape[2:], f32)
    for k in range(nz):
        up_grad = lax.dynamic_update_slice_in_dim(
            up_grad, z_blocks[k][:, None], lax.rem(z_i - k + nz, nz), axis=1
        )
    up_grad = up_grad.reshape(r_own, width)

    ungained = jnp.sum(arrived.astype(f32), axis=0)
    down_grad = ungained * gain[:, None]
    gain_grad = jnp.sum(ungained * adapter_down.astype(f32), axis=1)
    return (query_grad[None], passage_grad[None], down_grad, up_grad, gain_grad)


def solution(mesh):
    nyl, nyh, nc = 2, 2, 2
    nx, nz = mesh.shape["pb"] // nyl, mesh.shape["pa"] // (nyh * nc)
    sizes = (nx, nyl, nz, nyh, nc)
    fine = Mesh(mesh.devices.reshape(sizes), everyone)
    pb, pa = ("x", "yl"), ("z", "yh", "c")
    in_specs = (
        P(pb, pa, None),
        P(pa, pb, None),
        P(pb, pa),
        P(pb, pa, None, None),
        P(pa, pb, None, None),
        P(pb, pa, None),
        P(pa, pb, None),
        P(everyone),
        P(everyone, None),
        P(everyone, None),
    )
    out_specs = (P(pb, pa, None), P(pa, pb, None), P(everyone, None), P(everyone, None), P(everyone))

    def body(*args):
        return per_device(sizes, *args)

    return jax.shard_map(body, mesh=fine, in_specs=in_specs, out_specs=out_specs, check_vma=False)
```

```python
import jax
import jax.numpy as jnp
from jax import lax
from jax.experimental import pallas as pl
from jax.experimental.pallas import tpu as pltpu
from jax.sharding import Mesh, PartitionSpec as P

scale = 1.0 / 0.05
epsilon = 1e-06
bf16 = jnp.bfloat16
f32 = jnp.float32
everyone = ("x", "yl", "z", "yh", "c")
swap2 = [(0, 1), (1, 0)]
barrier = lax.optimization_barrier


def shift(value, axis, step, size):
    return lax.ppermute(value, axis, [(i, (i + step) % size) for i in range(size)])


def swap(value, axis):
    return lax.ppermute(value, axis, swap2)


def ring_sides(block, ring):
    return shift(block, ring, 1, 4), shift(block, ring, 3, 4)


def ring_far(before, after, ring):
    half = before.shape[0] // 2
    return shift(before[:half], ring, 1, 4), shift(after[half:], ring, 3, 4)


def ring_sum(parts, ring, size):
    return [parts[0]] + [shift(parts[k], ring, size - k, size) for k in range(1, size)]


def cut_rows(part, count):
    rows = part.shape[0] // count
    return [part[k * rows : (k + 1) * rows] for k in range(count)]


def add_up(terms):
    total = terms[0].astype(f32)
    for t in terms[1:]:
        total = total + t.astype(f32)
    return total


def pair_sum(total, pair):
    half = total.shape[0] // 2
    return (total[:half] + swap(total[half:].astype(bf16), pair).astype(f32)).astype(bf16)


gelu_root = 0.7978845608028654
gelu_cube = 0.044715
kernel_room = pltpu.CompilerParams(vmem_limit_bytes=60 * 1024 * 1024)
light = pl.CostEstimate(flops=0, bytes_accessed=0, transcendentals=0)
any_space = pl.BlockSpec(memory_space=pl.ANY)
in_vmem = pl.BlockSpec(memory_space=pltpu.VMEM)
in_smem = pl.BlockSpec(memory_space=pltpu.SMEM)


turned = (((0,), (0,)), ((), ()))
contract = (((1,), (1,)), ((), ()))


def load_blocks(parts, wholes, sems):
    copies, n = [], 0
    for blocks, whole in zip(parts, wholes):
        row = 0
        for block in blocks:
            copies.append(pltpu.make_async_copy(block, whole.at[pl.ds(row, block.shape[0])], sems.at[n]))
            row, n = row + block.shape[0], n + 1
    for c in copies:
        c.start()
    return copies


def wait_all(copies):
    for c in copies:
        c.wait()


def score_kernel(n_q, n_p, *refs):
    q_blocks, p_blocks = refs[:n_q], refs[n_q : n_q + n_p]
    scores, top, total, q_all, p_all, sems = refs[n_q + n_p :]
    wait_all(load_blocks((q_blocks, p_blocks), (q_all, p_all), sems))
    s = lax.dot_general(q_all[...], p_all[...], contract, preferred_element_type=f32) * scale
    scores[...] = s
    m = jnp.max(s, axis=1, keepdims=True)
    top[...] = m
    total[...] = jnp.sum(jnp.exp(s - m), axis=1, keepdims=True)


def rows_of(blocks):
    return sum(b.shape[0] for b in blocks)


def block_scratch(q_blocks, p_blocks):
    width = q_blocks[0].shape[1]
    return [
        pltpu.VMEM((rows_of(q_blocks), width), bf16),
        pltpu.VMEM((rows_of(p_blocks), width), bf16),
        pltpu.SemaphoreType.DMA((len(q_blocks) + len(p_blocks),)),
    ]


def score_block(q_blocks, p_blocks):
    n_q, n_p = rows_of(q_blocks), rows_of(p_blocks)
    column = jax.ShapeDtypeStruct((n_q, 1), f32)
    return pl.pallas_call(
        lambda *refs: score_kernel(len(q_blocks), len(p_blocks), *refs),
        out_shape=(jax.ShapeDtypeStruct((n_q, n_p), f32), column, column),
        in_specs=[any_space] * (len(q_blocks) + len(p_blocks)),
        out_specs=(in_vmem,) * 3,
        scratch_shapes=block_scratch(q_blocks, p_blocks),
        compiler_params=kernel_room,
        cost_estimate=light,
    )(*q_blocks, *p_blocks)


def couple_kernel(n_q, n_p, sizes, counts, spot, scores, stat, columns, *refs):
    q_blocks, p_blocks = refs[:n_q], refs[n_q : n_q + n_p]
    coupling, q_few, p_few, q_all, p_all, sems = refs[n_q + n_p :]
    copies = load_blocks((q_blocks, p_blocks), (q_all, p_all), sems)
    soft = jnp.exp(scores[...] - stat[:, 0:1]) / stat[:, 1:2]
    hit = (stat[:, 2:3].astype(jnp.int32) == columns[...]).astype(f32)
    link = (soft - hit).astype(bf16)
    coupling[...] = link
    wait_all(copies)
    rows, cols = link.shape
    nx, nyl, nz, nyh, nc = sizes
    yl, yh, core, x, z = (spot[k] for k in range(head))
    q_seqs, q_row, p_seqs, p_row = counts
    n_q_owners = q_few.shape[0]

    n_few = n_q_owners * q_seqs
    few_i = lax.broadcasted_iota(jnp.int32, (n_few, rows), 0)
    here = lax.broadcasted_iota(jnp.int32, (n_few, rows), 1)
    seq, owner = few_i % q_seqs, few_i // q_seqs
    step = (z - owner // nyh + nz) % nz * nyh + (yh - owner % nyh + nyh) % nyh
    pick = (here == step * q_row + seq).astype(bf16)
    first = jnp.dot(pick, link, preferred_element_type=f32).astype(bf16)
    found = jnp.dot(first, p_all[...], preferred_element_type=f32) * scale
    for k in range(n_q_owners):
        q_few[k] = found[k * q_seqs : (k + 1) * q_seqs].astype(bf16)

    n_few = p_few.shape[0] * p_seqs
    few_i = lax.broadcasted_iota(jnp.int32, (n_few, cols), 0)
    here = lax.broadcasted_iota(jnp.int32, (n_few, cols), 1)
    seq, owner = few_i % p_seqs, few_i // p_seqs
    x_step = (x - owner // (nyl * nc) + nx) % nx
    yl_step = (yl - owner // nc % nyl + nyl) % nyl
    core_step = (core - owner % nc + nc) % nc
    pick = (here == ((core_step * nx + x_step) * nyl + yl_step) * p_row + seq).astype(bf16)
    first = lax.dot_general(pick, link, contract, preferred_element_type=f32).astype(bf16)
    found = jnp.dot(first, q_all[...], preferred_element_type=f32) * scale
    for k in range(p_few.shape[0]):
        p_few[k] = found[k * p_seqs : (k + 1) * p_seqs].astype(bf16)


def couple(spot, scores, stat, columns, q_blocks, p_blocks, sizes, counts):
    n_q, n_p = scores.shape
    width = q_blocks[0].shape[1]
    q_seqs, q_row, p_seqs, p_row = counts
    return pl.pallas_call(
        lambda *refs: couple_kernel(len(q_blocks), len(p_blocks), sizes, counts, *refs),
        out_shape=(
            jax.ShapeDtypeStruct((n_q, n_p), bf16),
            jax.ShapeDtypeStruct((n_q // q_row, q_seqs, width), bf16),
            jax.ShapeDtypeStruct((n_p // p_row, p_seqs, width), bf16),
        ),
        in_specs=[in_smem] + [in_vmem] * 3 + [any_space] * (len(q_blocks) + len(p_blocks)),
        out_specs=[in_vmem] * 3,
        scratch_shapes=block_scratch(q_blocks, p_blocks),
        compiler_params=kernel_room,
        cost_estimate=light,
    )(spot, scores, stat, columns, *q_blocks, *p_blocks)


def ring_add_kernel(n, *refs):
    total = refs[0][...].astype(f32)
    for r in refs[1:n]:
        total = total + r[...].astype(f32)
    half = total.shape[0] // 2
    refs[n][...] = total[:half]
    refs[n + 1][...] = total[half:].astype(bf16)


def ring_add(terms):
    rows, width = terms[0].shape
    tile = width // 2

    def cut(n):
        return pl.BlockSpec((n, tile), lambda i: (0, i))

    return pl.pallas_call(
        lambda *refs: ring_add_kernel(len(terms), *refs),
        grid=(2,),
        out_shape=(jax.ShapeDtypeStruct((rows // 2, width), f32), jax.ShapeDtypeStruct((rows // 2, width), bf16)),
        in_specs=[cut(rows)] * len(terms),
        out_specs=(cut(rows // 2),) * 2,
        compiler_params=kernel_room,
        cost_estimate=pl.CostEstimate(
            flops=0, bytes_accessed=2 * rows * width * (len(terms) + 2), transcendentals=0
        ),
    )(*terms)


def core_add_kernel(n, *refs):
    for keep, came, out in zip(refs[:n], refs[n : 2 * n], refs[2 * n :]):
        out[...] = (keep[...].astype(f32) + came[...].astype(f32)).astype(bf16)


def core_add(keep, came):
    steps = 2
    width = keep[0].shape[-1]

    def cut(a):
        return pl.BlockSpec(a.shape[:-1] + (width // steps,), lambda i: (0,) * (a.ndim - 1) + (i,))

    return pl.pallas_call(
        lambda *refs: core_add_kernel(len(keep), *refs),
        grid=(steps,),
        out_shape=[jax.ShapeDtypeStruct(a.shape, bf16) for a in keep],
        in_specs=[cut(a) for a in (*keep, *came)],
        out_specs=[cut(a) for a in keep],
        compiler_params=kernel_room,
        cost_estimate=light,
    )(*keep, *came)


def chip_add_kernel(n, keep, *refs):
    out = refs[n]
    rows = refs[0].shape[0]
    for k in range(n):
        here = pl.ds(k * rows, rows)
        out[here] = (keep[here].astype(f32) + refs[k][...].astype(f32)).astype(bf16)


def chip_add(keep, came):
    steps = 2
    width = keep.shape[-1]

    def cut(a):
        return pl.BlockSpec(a.shape[:-1] + (width // steps,), lambda i: (0,) * (a.ndim - 1) + (i,))

    return pl.pallas_call(
        lambda *refs: chip_add_kernel(len(came), *refs),
        grid=(steps,),
        out_shape=jax.ShapeDtypeStruct(keep.shape, bf16),
        in_specs=[cut(keep)] + [cut(a) for a in came],
        out_specs=cut(keep),
        compiler_params=kernel_room,
        cost_estimate=light,
    )(keep, *came)


def parts_kernel(n_blocks, n_out, turn, coupling, *refs):
    blocks, outs = refs[:n_blocks], refs[n_blocks : n_blocks + n_out]
    link = coupling[...]
    rows = outs[0].shape[0]
    whole = jnp.concatenate([b[...] for b in blocks], axis=0)
    if turn:
        part = lax.dot_general(link, whole, turned, preferred_element_type=f32)
    else:
        part = jnp.dot(link, whole, preferred_element_type=f32)
    part = (part * scale).astype(bf16)
    for k in range(n_out):
        outs[k][...] = part[k * rows : (k + 1) * rows]


def grad_parts(coupling, blocks, n_out, turn):
    n_q, n_p = coupling.shape
    width = blocks[0].shape[1]
    tile = 2048
    rows = (n_p if turn else n_q) // n_out

    def cut(n):
        return pl.BlockSpec((n, tile), lambda i: (0, i))

    return pl.pallas_call(
        lambda *refs: parts_kernel(len(blocks), n_out, turn, *refs),
        grid=(width // tile,),
        out_shape=[jax.ShapeDtypeStruct((rows, width), bf16)] * n_out,
        in_specs=[pl.BlockSpec((n_q, n_p), lambda i: (0, 0))] + [cut(b.shape[0]) for b in blocks],
        out_specs=[cut(rows)] * n_out,
        compiler_params=kernel_room,
        cost_estimate=pl.CostEstimate(
            flops=2 * n_q * n_p * width, bytes_accessed=2 * (n_q + n_p) * width, transcendentals=0
        ),
    )(coupling, *blocks)


def down_kernel(core, tok_q, tok_p, inner_q, inner_p, keep, *gives):
    part = lax.dot_general(tok_p[...], inner_p[...], turned, preferred_element_type=f32)
    part = part + lax.dot_general(tok_q[...], inner_q[...], turned, preferred_element_type=f32)
    chips, rows, hidden = keep.shape
    part = part.astype(bf16).reshape(chips, 2, rows, hidden)
    first = core[2] == 0
    piece = pl.program_id(0) // (pl.num_programs(0) // len(gives))

    @pl.when(first)
    def _():
        keep[...] = part[:, 0]

    @pl.when(jnp.logical_not(first))
    def _():
        keep[...] = part[:, 1]

    for k, give in enumerate(gives):

        @pl.when((piece == k) & first)
        def _():
            give[...] = part[:, 1]

        @pl.when((piece == k) & jnp.logical_not(first))
        def _():
            give[...] = part[:, 0]


def down_parts(spot, tok_q, tok_p, inner_q, inner_p, rows):
    width, hidden = tok_q.shape[1], inner_q.shape[1]
    tile, pieces = 1024, 4
    chips = tile // (2 * rows)
    steps = width // tile
    each = steps // pieces
    n_chips = width // (2 * rows)

    def cut(a):
        return pl.BlockSpec((a.shape[0], tile), lambda i: (0, i))

    def piece_spec(k):
        return pl.BlockSpec((chips, rows, hidden), lambda i: (jnp.clip(i - k * each, 0, each - 1), 0, 0))

    out = pl.pallas_call(
        down_kernel,
        grid=(steps,),
        out_shape=[jax.ShapeDtypeStruct((n_chips, rows, hidden), bf16)]
        + [jax.ShapeDtypeStruct((n_chips // pieces, rows, hidden), bf16)] * pieces,
        in_specs=[
            in_smem, cut(tok_q), cut(tok_p),
            pl.BlockSpec(inner_q.shape, lambda i: (0, 0)), pl.BlockSpec(inner_p.shape, lambda i: (0, 0)),
        ],
        out_specs=[pl.BlockSpec((chips, rows, hidden), lambda i: (i, 0, 0))] + [piece_spec(k) for k in range(pieces)],
        compiler_params=kernel_room,
        cost_estimate=pl.CostEstimate(
            flops=2 * (tok_q.shape[0] + tok_p.shape[0]) * width * hidden, bytes_accessed=4 * width * hidden,
            transcendentals=0,
        ),
    )(spot, tok_q, tok_p, inner_q, inner_p)
    return out[0], out[1:]


ring_places = ((0, 0, 2), (1, 0, 2), (2, 0, 1), (2, 1, 1), (3, 0, 2))
head = 5


def token_kernel(n_seq, n_blocks, spot, *rest):
    blocks = rest[:n_blocks]
    tok_q, tok_p, slope_q, slope_p, sums, weights, sems = rest[n_blocks:]
    i = pl.program_id(0)

    @pl.when(i == 0)
    def _():
        copies = []
        for k in range(n_blocks):
            step, first, count = ring_places[k % len(ring_places)]
            x = lax.rem(spot[3] - step + 4, 4)
            core = lax.rem(spot[2] + k // len(ring_places), 2)
            copies.append(
                pltpu.make_async_copy(
                    blocks[k].at[:, :, :, pl.ds(0, weights.shape[5])],
                    weights.at[x, pl.ds(first, count), :, :, core],
                    sems.at[k],
                )
            )
        for c in copies:
            c.start()
        sums[...] = jnp.zeros_like(sums)
        for c in copies:
            c.wait()

    hidden = weights.shape[-1]

    def work(tok, slope, first_row):
        rows = tok.shape[0]
        wide = tok[...].astype(f32)
        inverse = lax.rsqrt(jnp.mean(wide * wide, axis=1, keepdims=True) + epsilon)
        pre = jnp.dot(tok[...], weights[...].reshape(-1, hidden), preferred_element_type=f32) * inverse
        square = pre * pre
        bend = jnp.tanh(gelu_root * pre * (1.0 + gelu_cube * square))
        up = 0.5 * (1.0 + bend)
        active = (pre * up).astype(bf16)
        steep = up + 0.5 * pre * (1.0 - bend * bend) * (gelu_root * (1.0 + 3.0 * gelu_cube * square))
        slope[...] = steep * inverse
        seq = lax.broadcasted_iota(jnp.int32, (sums.shape[0], rows), 0)
        row = lax.broadcasted_iota(jnp.int32, (sums.shape[0], rows), 1) + first_row
        member = jnp.zeros((sums.shape[0], rows), f32)
        for k in range(n_seq):
            inside = (row >= spot[head + k]) & (row < spot[head + n_seq + k]) & (seq == k)
            member = jnp.where(inside, 1.0, member)
        sums[...] += jnp.dot(member.astype(bf16), active, preferred_element_type=f32)

    @pl.when(i == 0)
    def _():
        work(tok_q, slope_q, 0)

    @pl.when(i > 0)
    def _():
        work(tok_p, slope_p, tok_q.shape[0] + (i - 1) * tok_p.shape[0])


def token_half(spot, blocks, tok_q, tok_p, n_seq, n_seq8):
    width = tok_q.shape[1]
    nyl, nz, nyh, both, hidden = blocks[0].shape
    d_own = width // (4 * nyl * nz * nyh * 2)
    steps = 2
    tile = tok_p.shape[0] // steps

    def tile_of(i):
        return (jnp.maximum(i - 1, 0), 0)

    return pl.pallas_call(
        lambda *refs: token_kernel(n_seq, len(blocks), *refs),
        grid=(steps + 1,),
        out_shape=(
            jax.ShapeDtypeStruct((tok_q.shape[0], hidden), f32),
            jax.ShapeDtypeStruct((tok_p.shape[0], hidden), f32),
            jax.ShapeDtypeStruct((n_seq8, hidden), f32),
        ),
        in_specs=[in_smem] + [any_space] * len(blocks)
        + [pl.BlockSpec(tok_q.shape, lambda i: (0, 0)), pl.BlockSpec((tile, width), tile_of)],
        out_specs=(
            pl.BlockSpec((tok_q.shape[0], hidden), lambda i: (0, 0)),
            pl.BlockSpec((tile, hidden), tile_of),
            pl.BlockSpec((n_seq8, hidden), lambda i: (0, 0)),
        ),
        scratch_shapes=[
            pltpu.VMEM((4, nyl, nz, nyh, 2, d_own, hidden), bf16), pltpu.SemaphoreType.DMA((len(blocks),))
        ],
        compiler_params=kernel_room,
        cost_estimate=light,
    )(spot, *blocks, tok_q, tok_p)


def hidden_kernel(n_blocks, units, grads, *refs):
    blocks = refs[:n_blocks]
    out, lines, sems = refs[n_blocks:]
    rows, line = lines.shape[-2:]
    copies = [
        pltpu.make_async_copy(
            blocks[k].at[:, :, :, pl.ds(blocks[k].shape[3] - rows, rows)],
            lines.at[step, pl.ds(first, count)],
            sems.at[k],
        )
        for k, (step, first, count) in enumerate(ring_places)
    ]
    for c in copies:
        c.start()
    n_seq, width = grads.shape
    per_unit = width // line
    cut = jnp.concatenate([grads[:, j * line : (j + 1) * line] for j in range(per_unit)], axis=0)
    for c in copies:
        c.wait()
    flat = lines[...].reshape(-1, line)
    found = lax.dot_general(cut, flat, contract, preferred_element_type=f32)
    which = lax.broadcasted_iota(jnp.int32, (n_seq, flat.shape[0]), 1) % per_unit
    kept = jnp.zeros((n_seq, flat.shape[0]), f32)
    for j in range(per_unit):
        kept = jnp.where(which == j, found[j * n_seq : (j + 1) * n_seq], kept)
    source = lax.broadcasted_iota(jnp.int32, (flat.shape[0], units), 0) // per_unit
    to = lax.broadcasted_iota(jnp.int32, (flat.shape[0], units), 1)
    gather = (source == to).astype(bf16)
    total = jnp.zeros((n_seq, units), f32)
    for _ in range(3):
        piece = kept.astype(bf16)
        total = total + jnp.dot(piece, gather, preferred_element_type=f32)
        kept = kept - piece.astype(f32)
    out[...] = total


def hidden_of(grads, blocks, rows, units):
    shape = blocks[0].shape
    return pl.pallas_call(
        lambda *refs: hidden_kernel(len(blocks), units, *refs),
        out_shape=jax.ShapeDtypeStruct((grads.shape[0], units), f32),
        in_specs=[in_vmem] + [any_space] * len(blocks),
        out_specs=in_vmem,
        scratch_shapes=[
            pltpu.VMEM((4,) + shape[:3] + (rows, shape[4]), bf16), pltpu.SemaphoreType.DMA((len(blocks),))
        ],
        compiler_params=kernel_room,
        cost_estimate=light,
    )(grads, *blocks)


def inner_kernel(n_seq, spot, own, other, order, slope_q, slope_p, inner_q, inner_p):
    found = jnp.concatenate([own[...], other[...]], axis=1)
    hidden = jnp.zeros_like(found)
    for _ in range(3):
        piece = found.astype(bf16)
        hidden = hidden + jnp.dot(piece, order[...], preferred_element_type=f32)
        found = found - piece.astype(f32)
    first_row = 0
    for slope, inner in ((slope_q, inner_q), (slope_p, inner_p)):
        row = lax.broadcasted_iota(jnp.int32, (slope.shape[0], 1), 0) + first_row
        spread_out = jnp.zeros(slope.shape, f32)
        for k in range(n_seq):
            inside = (row >= spot[head + k]) & (row < spot[head + n_seq + k])
            spread_out = jnp.where(inside, hidden[k : k + 1, :], spread_out)
        inner[...] = (slope[...] * spread_out).astype(bf16)
        first_row += slope.shape[0]


def inner_of(spot, own, other, order, slope_q, slope_p, n_seq):
    return pl.pallas_call(
        lambda *refs: inner_kernel(n_seq, *refs),
        out_shape=(jax.ShapeDtypeStruct(slope_q.shape, bf16), jax.ShapeDtypeStruct(slope_p.shape, bf16)),
        in_specs=[in_smem] + [in_vmem] * 5,
        out_specs=(in_vmem,) * 2,
        compiler_params=kernel_room,
        cost_estimate=light,
    )(spot, own, other, order, slope_q, slope_p)


def spread(block, axes, count):
    return lax.all_to_all(jnp.broadcast_to(block[None], (count,) + block.shape), axes, 0, 0)


def per_device(sizes, query_cache, passage_cache, positive, query_tokens, passage_tokens,
               query_lengths, passage_lengths, norm_gain, adapter_down, adapter_up):
    nx, nyl, nz, nyh, nc = sizes
    n_all = nx * nyl * nz * nyh * nc
    n_pb, n_pa = nx * nyl, nz * nyh * nc
    x_i, yl_i, z_i, yh_i, c_i = (lax.axis_index(a) for a in everyone)
    first_core = c_i == 0
    own_queries, own_passages = query_cache[0], passage_cache[0]
    width = own_queries.shape[1]
    qrow, prow = own_queries.shape[0], own_passages.shape[0]
    d_own, hidden_width = adapter_down.shape
    r_own = adapter_up.shape[0]
    q_seqs, p_seqs = query_lengths.shape[-1], passage_lengths.shape[-1]

    chips = ("x", "yl", "z", "yh")
    n_chips = n_all // nc
    gain = norm_gain.astype(f32)
    gained_down = (adapter_down.astype(f32) * gain[:, None]).astype(bf16)
    (q_next, p_next, gained_down, adapter_up, query_lengths, passage_lengths, yl_i, yh_i, c_i) = barrier(
        (swap(own_queries, "yh"), swap(own_passages, "yl"), gained_down, adapter_up,
         query_lengths, passage_lengths, yl_i, yh_i, c_i)
    )

    q_pair = jnp.concatenate([own_queries, q_next], axis=0)
    p_pair = jnp.concatenate([own_passages, p_next], axis=0)
    q_before, q_after = ring_sides(q_pair, "z")
    p_before, p_after = ring_sides(p_pair, "x")
    q_blocks = [q_pair, q_before, *ring_far(q_before, q_after, "z"), q_after]
    p_blocks = [p_pair, p_before, *ring_far(p_before, p_after, "x"), p_after]
    p_other = swap(p_pair, "c")

    tok_q, tok_p = query_tokens[0, 0], passage_tokens[0, 0]
    lengths = jnp.concatenate([query_lengths[0, 0], passage_lengths[0, 0]], axis=0)
    n_seq = lengths.shape[0]
    pad = -n_seq % 8
    n_seq8 = n_seq + pad
    ends = jnp.cumsum(lengths)
    spot = jnp.concatenate([jnp.stack([yl_i, yh_i, c_i, x_i, z_i]), ends - lengths, ends]).astype(jnp.int32)

    here = jnp.arange(hidden_width, dtype=jnp.int32)
    unit, rest = here % r_own, here // r_own
    yh_s, rest = rest % nyh, rest // nyh
    z_s, rest = rest % nz, rest // nz
    yl_s, rest = rest % nyl, rest // nyl
    x_s, c_s = lax.rem(x_i - rest % nx + nx, nx), lax.rem(c_i + rest // nx, nc)
    place = ((((x_s * nyl + yl_s) * nz + z_s) * nyh + yh_s) * nc + c_s) * r_own + unit
    order = (place[:, None] == here[None, :]).astype(bf16)

    q_blocks, p_blocks, p_other, spot, order, gained_down, adapter_up = barrier(
        (q_blocks, p_blocks, p_other, spot, order, gained_down, adapter_up)
    )
    near = spread(
        jnp.concatenate([gained_down, adapter_up.reshape(-1, hidden_width)], axis=0),
        ("yl", "z", "yh"), nyl * nz * nyh,
    ).reshape(nyl, nz, nyh, -1, hidden_width)
    p_blocks = barrier(p_blocks + [p_other] + [swap(b, "c") for b in p_blocks[1:]])

    scores, local_top, local_sum = score_block(q_blocks, p_blocks)

    m_i = z_i * nyh + yh_i
    groups = nz * nyh
    step = jnp.arange(groups, dtype=jnp.int32)
    owner = lax.rem(z_i - step // nyh + nz, nz) * nyh + lax.rem(yh_i - step % nyh + nyh, nyh)
    pick = owner[:, None] == step[None, :]

    def to_owner(v):
        return jnp.sum(jnp.where(pick[:, :, None], v.reshape(groups, 1, qrow), 0), axis=0)

    def to_step(v):
        return jnp.sum(jnp.where(pick[:, :, None], v.reshape(1, groups, qrow), 0), axis=1).reshape(-1)

    packet = jnp.concatenate(
        [to_owner(local_top).reshape(-1), to_owner(local_sum).reshape(-1), positive[0].astype(f32)]
    )
    packet = jnp.pad(packet, (0, -packet.shape[0] % 128))
    packet, near = barrier((packet, near))
    near_down, near_up = near[:, :, :, :d_own], near[:, :, :, d_own:]
    down_before, down_after = ring_sides(near_down, "x")
    up_before, up_after = ring_sides(near_up, "x")
    stats = spread(packet, ("z", "yh"), groups)

    stats, down_before, down_after = barrier((stats, down_before, down_after))
    down_far = ring_far(down_before, down_after, "x")
    n_q = groups * qrow
    tops, sums = stats[:, :n_q], stats[:, n_q : 2 * n_q]
    row_top = jnp.max(tops, axis=0)
    row_sum = jnp.sum(sums * jnp.exp(tops - row_top[None, :]), axis=0)
    target = stats[:, 2 * n_q : 2 * n_q + qrow]
    stat = jnp.stack([to_step(row_top), to_step(row_sum), to_step(target)], axis=1)

    core_step = jnp.arange(nc, dtype=jnp.int32)[:, None, None, None]
    x_step = jnp.arange(nx, dtype=jnp.int32)[None, :, None, None]
    yl_step = jnp.arange(nyl, dtype=jnp.int32)[None, None, :, None]
    lane = jnp.arange(prow, dtype=jnp.int32)[None, None, None, :]
    a_of = m_i * nc + lax.rem(c_i + core_step, nc)
    b_of = lax.rem(x_i - x_step + nx, nx) * nyl + lax.rem(yl_i - yl_step + nyl, nyl)
    columns = (a_of * (n_pb * prow) + b_of * prow + lane).reshape(-1)

    coupling, q_few, p_few = couple(
        spot, scores, stat, columns[None, :], q_blocks, p_blocks, sizes, (q_seqs, qrow, p_seqs, prow)
    )
    p_few = lax.all_to_all(p_few, ("x", "yl", "c"), 0, 0)
    q_few = lax.all_to_all(q_few, ("z", "yh"), 0, 0)

    q_part = grad_parts(coupling, p_blocks, nz, False)
    coupling, q_few, q_part, up_before, up_after = barrier((coupling, q_few, q_part, up_before, up_after))
    p_part = grad_parts(coupling, q_blocks, nc * nx, True)
    p_keep, p_give = p_part[:nx], p_part[nx:]

    p_few, p_keep, p_give, down_far, up_before, up_after, q_terms = barrier(
        (p_few, p_keep, p_give, down_far, up_before, up_after, ring_sum(q_part, "z", nz))
    )
    up_far = ring_far(up_before, up_after, "x")
    down_x = [near_down, down_before, *down_far, down_after]
    up_x = [near_up, up_before, *up_far, up_after]

    p_sum = core_add(p_keep, [swap(b, "c") for b in p_give])
    down_blocks, p_sum, up_x = barrier((down_x + [swap(b, "c") for b in down_x], p_sum, up_x))
    slope_q, slope_p, active_sums = token_half(spot, down_blocks, tok_q, tok_p, n_seq, n_seq8)
    r_block, d_block = hidden_width // n_pb, width // n_pa
    sum_blocks = active_sums.astype(bf16).reshape(n_seq8, n_pb, r_block).transpose(1, 0, 2)
    sum_blocks = jnp.pad(sum_blocks, ((0, 0), (0, 0), (0, -r_block % 128)))
    q_few = jnp.sum(q_few.astype(f32), axis=0).astype(bf16)
    p_few = jnp.sum(p_few.astype(f32), axis=0).astype(bf16)

    emb_grads = jnp.concatenate([q_few, p_few], axis=0).astype(f32)
    seq_grads = (emb_grads / lengths.astype(f32)[:, None]).astype(bf16)
    seq_grads = jnp.pad(seq_grads, ((0, pad), (0, 0)))

    grad_blocks = seq_grads.reshape(n_seq8, n_pa, d_block).transpose(1, 0, 2)
    packet = jnp.concatenate(
        [
            jnp.broadcast_to(grad_blocks[None], (n_pb,) + grad_blocks.shape),
            jnp.broadcast_to(sum_blocks[:, None], (n_pb, n_pa) + sum_blocks.shape[1:]),
        ],
        axis=-1,
    ).reshape(n_all, n_seq8, -1)

    seq_both = jnp.concatenate([seq_grads, swap(seq_grads, "c")], axis=0)
    p_terms = ring_sum(p_sum, "x", nx)

    hidden = hidden_of(seq_both, up_x, r_own * width // hidden_width, hidden_width // nc)
    inner_q, inner_p = inner_of(
        spot, hidden[:n_seq8], swap(hidden[n_seq8:], "c"), order, slope_q, slope_p, n_seq
    )
    inner_q, inner_p, p_terms, packet = barrier((inner_q, inner_p, p_terms, packet))
    everything = lax.all_to_all(packet, everyone, 0, 0).reshape(n_all * n_seq8, -1)
    q_own, q_away = ring_add(q_terms)
    p_own, p_away = ring_add(p_terms)
    keep, give = down_parts(spot, tok_q, tok_p, inner_q, inner_p, d_own)
    keep, give, q_own, q_away, p_own, p_away, everything = barrier(
        (keep, give, q_own, q_away, p_own, p_away, everything)
    )
    chip_sum = chip_add(keep, [swap(b, "c") for b in give])
    up_block = lax.dot_general(
        everything[:, d_block : d_block + r_block], everything[:, :d_block], turned, preferred_element_type=f32
    ).reshape(nz, nyh, nc, r_own, 1, d_block)

    def trade(block, axis, index):
        first = index == 0
        mine = jnp.where(first, block[..., 0, :, :, :], block[..., 1, :, :, :])
        theirs = swap(jnp.where(first, block[..., 1, :, :, :], block[..., 0, :, :, :]), axis)
        return jnp.concatenate(
            [jnp.where(first, mine, theirs), jnp.where(first, theirs, mine)], axis=-2
        )

    up_block = trade(trade(up_block, "c", c_i), "yh", yh_i)
    z_blocks = [lax.dynamic_index_in_dim(up_block, lax.rem(z_i + k, nz), 0, keepdims=False) for k in range(nz)]
    z_blocks = [z_blocks[0]] + [shift(z_blocks[k], "z", k, nz) for k in range(1, nz)]
    chip_sum, z_blocks = barrier((chip_sum, z_blocks))
    query_grad = (q_own + swap(q_away, "yh").astype(f32)).astype(bf16)
    passage_grad = (p_own + swap(p_away, "yl").astype(f32)).astype(bf16)
    arrived = lax.all_to_all(chip_sum, chips, 0, 0)

    up_grad = jnp.zeros((r_own, nz) + up_block.shape[2:], f32)
    for k in range(nz):
        up_grad = lax.dynamic_update_slice_in_dim(
            up_grad, z_blocks[k][:, None], lax.rem(z_i - k + nz, nz), axis=1
        )
    up_grad = up_grad.reshape(r_own, width)

    ungained = jnp.sum(arrived.astype(f32), axis=0)
    down_grad = ungained * gain[:, None]
    gain_grad = jnp.sum(ungained * adapter_down.astype(f32), axis=1)
    return (query_grad[None], passage_grad[None], down_grad, up_grad, gain_grad)


def solution(mesh):
    nyl, nyh, nc = 2, 2, 2
    nx, nz = mesh.shape["pb"] // nyl, mesh.shape["pa"] // (nyh * nc)
    sizes = (nx, nyl, nz, nyh, nc)
    fine = Mesh(mesh.devices.reshape(sizes), everyone)
    pb, pa = ("x", "yl"), ("z", "yh", "c")
    in_specs = (
        P(pb, pa, None),
        P(pa, pb, None),
        P(pb, pa),
        P(pb, pa, None, None),
        P(pa, pb, None, None),
        P(pb, pa, None),
        P(pa, pb, None),
        P(everyone),
        P(everyone, None),
        P(everyone, None),
    )
    out_specs = (P(pb, pa, None), P(pa, pb, None), P(everyone, None), P(everyone, None), P(everyone))

    def body(*args):
        return per_device(sizes, *args)

    return jax.shard_map(body, mesh=fine, in_specs=in_specs, out_specs=out_specs, check_vma=False)
```

```python
import jax
import jax.numpy as jnp
from jax import lax
from jax.experimental import pallas as pl
from jax.experimental.pallas import tpu as pltpu
from jax.sharding import Mesh, PartitionSpec as P

scale = 1.0 / 0.05
epsilon = 1e-06
bf16 = jnp.bfloat16
f32 = jnp.float32
everyone = ("x", "yl", "z", "yh", "c")
swap2 = [(0, 1), (1, 0)]
barrier = lax.optimization_barrier


def shift(value, axis, step, size):
    return lax.ppermute(value, axis, [(i, (i + step) % size) for i in range(size)])


def swap(value, axis):
    return lax.ppermute(value, axis, swap2)


def ring_sides(block, ring):
    return shift(block, ring, 1, 4), shift(block, ring, 3, 4)


def ring_far(before, after, ring):
    half = before.shape[0] // 2
    return shift(before[:half], ring, 1, 4), shift(after[half:], ring, 3, 4)


def ring_sum(parts, ring, size):
    return [parts[0]] + [shift(parts[k], ring, size - k, size) for k in range(1, size)]


def cut_rows(part, count):
    rows = part.shape[0] // count
    return [part[k * rows : (k + 1) * rows] for k in range(count)]


def add_up(terms):
    total = terms[0].astype(f32)
    for t in terms[1:]:
        total = total + t.astype(f32)
    return total


def pair_sum(total, pair):
    half = total.shape[0] // 2
    return (total[:half] + swap(total[half:].astype(bf16), pair).astype(f32)).astype(bf16)


gelu_root = 0.7978845608028654
gelu_cube = 0.044715
kernel_room = pltpu.CompilerParams(vmem_limit_bytes=60 * 1024 * 1024)
light = pl.CostEstimate(flops=0, bytes_accessed=0, transcendentals=0)
any_space = pl.BlockSpec(memory_space=pl.ANY)
in_vmem = pl.BlockSpec(memory_space=pltpu.VMEM)
in_smem = pl.BlockSpec(memory_space=pltpu.SMEM)


turned = (((0,), (0,)), ((), ()))
contract = (((1,), (1,)), ((), ()))


def load_blocks(parts, wholes, sems):
    copies, n = [], 0
    for blocks, whole in zip(parts, wholes):
        row = 0
        for block in blocks:
            copies.append(pltpu.make_async_copy(block, whole.at[pl.ds(row, block.shape[0])], sems.at[n]))
            row, n = row + block.shape[0], n + 1
    for c in copies:
        c.start()
    return copies


def wait_all(copies):
    for c in copies:
        c.wait()


def score_kernel(n_q, n_p, *refs):
    q_blocks, p_blocks = refs[:n_q], refs[n_q : n_q + n_p]
    scores, top, total, q_all, p_all, sems = refs[n_q + n_p :]
    wait_all(load_blocks((q_blocks, p_blocks), (q_all, p_all), sems))
    s = lax.dot_general(q_all[...], p_all[...], contract, preferred_element_type=f32) * scale
    scores[...] = s
    m = jnp.max(s, axis=1, keepdims=True)
    top[...] = m
    total[...] = jnp.sum(jnp.exp(s - m), axis=1, keepdims=True)


def rows_of(blocks):
    return sum(b.shape[0] for b in blocks)


def block_scratch(q_blocks, p_blocks):
    width = q_blocks[0].shape[1]
    return [
        pltpu.VMEM((rows_of(q_blocks), width), bf16),
        pltpu.VMEM((rows_of(p_blocks), width), bf16),
        pltpu.SemaphoreType.DMA((len(q_blocks) + len(p_blocks),)),
    ]


def score_block(q_blocks, p_blocks):
    n_q, n_p = rows_of(q_blocks), rows_of(p_blocks)
    column = jax.ShapeDtypeStruct((n_q, 1), f32)
    return pl.pallas_call(
        lambda *refs: score_kernel(len(q_blocks), len(p_blocks), *refs),
        out_shape=(jax.ShapeDtypeStruct((n_q, n_p), f32), column, column),
        in_specs=[any_space] * (len(q_blocks) + len(p_blocks)),
        out_specs=(in_vmem,) * 3,
        scratch_shapes=block_scratch(q_blocks, p_blocks),
        compiler_params=kernel_room,
        cost_estimate=light,
    )(*q_blocks, *p_blocks)


def couple_kernel(n_q, n_p, sizes, counts, spot, scores, stat, columns, *refs):
    q_blocks, p_blocks = refs[:n_q], refs[n_q : n_q + n_p]
    coupling, q_few, p_few, q_all, p_all, sems = refs[n_q + n_p :]
    copies = load_blocks((q_blocks, p_blocks), (q_all, p_all), sems)
    soft = jnp.exp(scores[...] - stat[:, 0:1]) / stat[:, 1:2]
    hit = (stat[:, 2:3].astype(jnp.int32) == columns[...]).astype(f32)
    link = (soft - hit).astype(bf16)
    coupling[...] = link
    wait_all(copies)
    rows, cols = link.shape
    nx, nyl, nz, nyh, nc = sizes
    yl, yh, core, x, z = (spot[k] for k in range(head))
    q_seqs, q_row, p_seqs, p_row = counts
    n_q_owners = q_few.shape[0]

    n_few = n_q_owners * q_seqs
    few_i = lax.broadcasted_iota(jnp.int32, (n_few, rows), 0)
    here = lax.broadcasted_iota(jnp.int32, (n_few, rows), 1)
    seq, owner = few_i % q_seqs, few_i // q_seqs
    step = (z - owner // nyh + nz) % nz * nyh + (yh - owner % nyh + nyh) % nyh
    pick = (here == step * q_row + seq).astype(bf16)
    first = jnp.dot(pick, link, preferred_element_type=f32).astype(bf16)
    found = jnp.dot(first, p_all[...], preferred_element_type=f32) * scale
    for k in range(n_q_owners):
        q_few[k] = found[k * q_seqs : (k + 1) * q_seqs].astype(bf16)

    n_few = p_few.shape[0] * p_seqs
    few_i = lax.broadcasted_iota(jnp.int32, (n_few, cols), 0)
    here = lax.broadcasted_iota(jnp.int32, (n_few, cols), 1)
    seq, owner = few_i % p_seqs, few_i // p_seqs
    x_step = (x - owner // (nyl * nc) + nx) % nx
    yl_step = (yl - owner // nc % nyl + nyl) % nyl
    core_step = (core - owner % nc + nc) % nc
    pick = (here == ((core_step * nx + x_step) * nyl + yl_step) * p_row + seq).astype(bf16)
    first = lax.dot_general(pick, link, contract, preferred_element_type=f32).astype(bf16)
    found = jnp.dot(first, q_all[...], preferred_element_type=f32) * scale
    for k in range(p_few.shape[0]):
        p_few[k] = found[k * p_seqs : (k + 1) * p_seqs].astype(bf16)


def couple(spot, scores, stat, columns, q_blocks, p_blocks, sizes, counts):
    n_q, n_p = scores.shape
    width = q_blocks[0].shape[1]
    q_seqs, q_row, p_seqs, p_row = counts
    return pl.pallas_call(
        lambda *refs: couple_kernel(len(q_blocks), len(p_blocks), sizes, counts, *refs),
        out_shape=(
            jax.ShapeDtypeStruct((n_q, n_p), bf16),
            jax.ShapeDtypeStruct((n_q // q_row, q_seqs, width), bf16),
            jax.ShapeDtypeStruct((n_p // p_row, p_seqs, width), bf16),
        ),
        in_specs=[in_smem] + [in_vmem] * 3 + [any_space] * (len(q_blocks) + len(p_blocks)),
        out_specs=[in_vmem] * 3,
        scratch_shapes=block_scratch(q_blocks, p_blocks),
        compiler_params=kernel_room,
        cost_estimate=light,
    )(spot, scores, stat, columns, *q_blocks, *p_blocks)


def ring_add_kernel(n, *refs):
    total = refs[0][...].astype(f32)
    for r in refs[1:n]:
        total = total + r[...].astype(f32)
    half = total.shape[0] // 2
    refs[n][...] = total[:half]
    refs[n + 1][...] = total[half:].astype(bf16)


def ring_add(terms):
    rows, width = terms[0].shape
    tile = width // 2

    def cut(n):
        return pl.BlockSpec((n, tile), lambda i: (0, i))

    return pl.pallas_call(
        lambda *refs: ring_add_kernel(len(terms), *refs),
        grid=(2,),
        out_shape=(jax.ShapeDtypeStruct((rows // 2, width), f32), jax.ShapeDtypeStruct((rows // 2, width), bf16)),
        in_specs=[cut(rows)] * len(terms),
        out_specs=(cut(rows // 2),) * 2,
        compiler_params=kernel_room,
        cost_estimate=pl.CostEstimate(
            flops=0, bytes_accessed=2 * rows * width * (len(terms) + 2), transcendentals=0
        ),
    )(*terms)


def core_add_kernel(n, *refs):
    for keep, came, out in zip(refs[:n], refs[n : 2 * n], refs[2 * n :]):
        out[...] = (keep[...].astype(f32) + came[...].astype(f32)).astype(bf16)


def core_add(keep, came):
    steps = 2
    width = keep[0].shape[-1]

    def cut(a):
        return pl.BlockSpec(a.shape[:-1] + (width // steps,), lambda i: (0,) * (a.ndim - 1) + (i,))

    return pl.pallas_call(
        lambda *refs: core_add_kernel(len(keep), *refs),
        grid=(steps,),
        out_shape=[jax.ShapeDtypeStruct(a.shape, bf16) for a in keep],
        in_specs=[cut(a) for a in (*keep, *came)],
        out_specs=[cut(a) for a in keep],
        compiler_params=kernel_room,
        cost_estimate=light,
    )(*keep, *came)


def chip_add_kernel(n, keep, *refs):
    out = refs[n]
    rows = refs[0].shape[0]
    for k in range(n):
        here = pl.ds(k * rows, rows)
        out[here] = (keep[here].astype(f32) + refs[k][...].astype(f32)).astype(bf16)


def chip_add(keep, came):
    steps = 2
    width = keep.shape[-1]

    def cut(a):
        return pl.BlockSpec(a.shape[:-1] + (width // steps,), lambda i: (0,) * (a.ndim - 1) + (i,))

    return pl.pallas_call(
        lambda *refs: chip_add_kernel(len(came), *refs),
        grid=(steps,),
        out_shape=jax.ShapeDtypeStruct(keep.shape, bf16),
        in_specs=[cut(keep)] + [cut(a) for a in came],
        out_specs=cut(keep),
        compiler_params=kernel_room,
        cost_estimate=light,
    )(keep, *came)


def parts_kernel(n_blocks, n_out, turn, coupling, *refs):
    blocks, outs = refs[:n_blocks], refs[n_blocks : n_blocks + n_out]
    link = coupling[...]
    rows = outs[0].shape[0]
    whole = jnp.concatenate([b[...] for b in blocks], axis=0)
    if turn:
        part = lax.dot_general(link, whole, turned, preferred_element_type=f32)
    else:
        part = jnp.dot(link, whole, preferred_element_type=f32)
    part = (part * scale).astype(bf16)
    for k in range(n_out):
        outs[k][...] = part[k * rows : (k + 1) * rows]


def grad_parts(coupling, blocks, n_out, turn):
    n_q, n_p = coupling.shape
    width = blocks[0].shape[1]
    tile = 2048
    rows = (n_p if turn else n_q) // n_out

    def cut(n):
        return pl.BlockSpec((n, tile), lambda i: (0, i))

    return pl.pallas_call(
        lambda *refs: parts_kernel(len(blocks), n_out, turn, *refs),
        grid=(width // tile,),
        out_shape=[jax.ShapeDtypeStruct((rows, width), bf16)] * n_out,
        in_specs=[pl.BlockSpec((n_q, n_p), lambda i: (0, 0))] + [cut(b.shape[0]) for b in blocks],
        out_specs=[cut(rows)] * n_out,
        compiler_params=kernel_room,
        cost_estimate=pl.CostEstimate(
            flops=2 * n_q * n_p * width, bytes_accessed=2 * (n_q + n_p) * width, transcendentals=0
        ),
    )(coupling, *blocks)


def down_kernel(core, tok_q, tok_p, inner_q, inner_p, keep, *gives):
    part = lax.dot_general(tok_p[...], inner_p[...], turned, preferred_element_type=f32)
    part = part + lax.dot_general(tok_q[...], inner_q[...], turned, preferred_element_type=f32)
    chips, rows, hidden = keep.shape
    part = part.astype(bf16).reshape(chips, 2, rows, hidden)
    first = core[2] == 0
    piece = pl.program_id(0) // (pl.num_programs(0) // len(gives))

    @pl.when(first)
    def _():
        keep[...] = part[:, 0]

    @pl.when(jnp.logical_not(first))
    def _():
        keep[...] = part[:, 1]

    for k, give in enumerate(gives):

        @pl.when((piece == k) & first)
        def _():
            give[...] = part[:, 1]

        @pl.when((piece == k) & jnp.logical_not(first))
        def _():
            give[...] = part[:, 0]


def down_parts(spot, tok_q, tok_p, inner_q, inner_p, rows):
    width, hidden = tok_q.shape[1], inner_q.shape[1]
    tile, pieces = 1024, 4
    chips = tile // (2 * rows)
    steps = width // tile
    each = steps // pieces
    n_chips = width // (2 * rows)

    def cut(a):
        return pl.BlockSpec((a.shape[0], tile), lambda i: (0, i))

    def piece_spec(k):
        return pl.BlockSpec((chips, rows, hidden), lambda i: (jnp.clip(i - k * each, 0, each - 1), 0, 0))

    out = pl.pallas_call(
        down_kernel,
        grid=(steps,),
        out_shape=[jax.ShapeDtypeStruct((n_chips, rows, hidden), bf16)]
        + [jax.ShapeDtypeStruct((n_chips // pieces, rows, hidden), bf16)] * pieces,
        in_specs=[
            in_smem, cut(tok_q), cut(tok_p),
            pl.BlockSpec(inner_q.shape, lambda i: (0, 0)), pl.BlockSpec(inner_p.shape, lambda i: (0, 0)),
        ],
        out_specs=[pl.BlockSpec((chips, rows, hidden), lambda i: (i, 0, 0))] + [piece_spec(k) for k in range(pieces)],
        compiler_params=kernel_room,
        cost_estimate=pl.CostEstimate(
            flops=2 * (tok_q.shape[0] + tok_p.shape[0]) * width * hidden, bytes_accessed=4 * width * hidden,
            transcendentals=0,
        ),
    )(spot, tok_q, tok_p, inner_q, inner_p)
    return out[0], out[1:]


ring_places = ((0, 0, 2), (1, 0, 2), (2, 0, 1), (2, 1, 1), (3, 0, 2))
head = 5


def token_kernel(n_seq, n_blocks, spot, *rest):
    blocks = rest[:n_blocks]
    tok_q, tok_p, slope_q, slope_p, sums, weights, sems = rest[n_blocks:]
    i = pl.program_id(0)

    @pl.when(i == 0)
    def _():
        copies = []
        for k in range(n_blocks):
            step, first, count = ring_places[k % len(ring_places)]
            x = lax.rem(spot[3] - step + 4, 4)
            core = lax.rem(spot[2] + k // len(ring_places), 2)
            copies.append(
                pltpu.make_async_copy(
                    blocks[k].at[:, :, :, pl.ds(0, weights.shape[5])],
                    weights.at[x, pl.ds(first, count), :, :, core],
                    sems.at[k],
                )
            )
        for c in copies:
            c.start()
        sums[...] = jnp.zeros_like(sums)
        for c in copies:
            c.wait()

    hidden = weights.shape[-1]

    def work(tok, slope, first_row):
        rows = tok.shape[0]
        wide = tok[...].astype(f32)
        inverse = lax.rsqrt(jnp.mean(wide * wide, axis=1, keepdims=True) + epsilon)
        pre = jnp.dot(tok[...], weights[...].reshape(-1, hidden), preferred_element_type=f32) * inverse
        square = pre * pre
        bend = jnp.tanh(gelu_root * pre * (1.0 + gelu_cube * square))
        up = 0.5 * (1.0 + bend)
        active = (pre * up).astype(bf16)
        steep = up + 0.5 * pre * (1.0 - bend * bend) * (gelu_root * (1.0 + 3.0 * gelu_cube * square))
        slope[...] = steep * inverse
        seq = lax.broadcasted_iota(jnp.int32, (sums.shape[0], rows), 0)
        row = lax.broadcasted_iota(jnp.int32, (sums.shape[0], rows), 1) + first_row
        member = jnp.zeros((sums.shape[0], rows), f32)
        for k in range(n_seq):
            inside = (row >= spot[head + k]) & (row < spot[head + n_seq + k]) & (seq == k)
            member = jnp.where(inside, 1.0, member)
        sums[...] += jnp.dot(member.astype(bf16), active, preferred_element_type=f32)

    @pl.when(i == 0)
    def _():
        work(tok_q, slope_q, 0)

    @pl.when(i > 0)
    def _():
        work(tok_p, slope_p, tok_q.shape[0] + (i - 1) * tok_p.shape[0])


def token_half(spot, blocks, tok_q, tok_p, n_seq, n_seq8):
    width = tok_q.shape[1]
    nyl, nz, nyh, both, hidden = blocks[0].shape
    d_own = width // (4 * nyl * nz * nyh * 2)
    steps = 2
    tile = tok_p.shape[0] // steps

    def tile_of(i):
        return (jnp.maximum(i - 1, 0), 0)

    return pl.pallas_call(
        lambda *refs: token_kernel(n_seq, len(blocks), *refs),
        grid=(steps + 1,),
        out_shape=(
            jax.ShapeDtypeStruct((tok_q.shape[0], hidden), f32),
            jax.ShapeDtypeStruct((tok_p.shape[0], hidden), f32),
            jax.ShapeDtypeStruct((n_seq8, hidden), f32),
        ),
        in_specs=[in_smem] + [any_space] * len(blocks)
        + [pl.BlockSpec(tok_q.shape, lambda i: (0, 0)), pl.BlockSpec((tile, width), tile_of)],
        out_specs=(
            pl.BlockSpec((tok_q.shape[0], hidden), lambda i: (0, 0)),
            pl.BlockSpec((tile, hidden), tile_of),
            pl.BlockSpec((n_seq8, hidden), lambda i: (0, 0)),
        ),
        scratch_shapes=[
            pltpu.VMEM((4, nyl, nz, nyh, 2, d_own, hidden), bf16), pltpu.SemaphoreType.DMA((len(blocks),))
        ],
        compiler_params=kernel_room,
        cost_estimate=light,
    )(spot, *blocks, tok_q, tok_p)


def hidden_kernel(n_blocks, units, grads, *refs):
    blocks = refs[:n_blocks]
    out, lines, sems = refs[n_blocks:]
    rows, line = lines.shape[-2:]
    copies = [
        pltpu.make_async_copy(
            blocks[k].at[:, :, :, pl.ds(blocks[k].shape[3] - rows, rows)],
            lines.at[step, pl.ds(first, count)],
            sems.at[k],
        )
        for k, (step, first, count) in enumerate(ring_places)
    ]
    for c in copies:
        c.start()
    n_seq, width = grads.shape
    per_unit = width // line
    cut = jnp.concatenate([grads[:, j * line : (j + 1) * line] for j in range(per_unit)], axis=0)
    for c in copies:
        c.wait()
    flat = lines[...].reshape(-1, line)
    found = lax.dot_general(cut, flat, contract, preferred_element_type=f32)
    which = lax.broadcasted_iota(jnp.int32, (n_seq, flat.shape[0]), 1) % per_unit
    kept = jnp.zeros((n_seq, flat.shape[0]), f32)
    for j in range(per_unit):
        kept = jnp.where(which == j, found[j * n_seq : (j + 1) * n_seq], kept)
    source = lax.broadcasted_iota(jnp.int32, (flat.shape[0], units), 0) // per_unit
    to = lax.broadcasted_iota(jnp.int32, (flat.shape[0], units), 1)
    gather = (source == to).astype(bf16)
    total = jnp.zeros((n_seq, units), f32)
    for _ in range(3):
        piece = kept.astype(bf16)
        total = total + jnp.dot(piece, gather, preferred_element_type=f32)
        kept = kept - piece.astype(f32)
    out[...] = total


def hidden_of(grads, blocks, rows, units):
    shape = blocks[0].shape
    return pl.pallas_call(
        lambda *refs: hidden_kernel(len(blocks), units, *refs),
        out_shape=jax.ShapeDtypeStruct((grads.shape[0], units), f32),
        in_specs=[in_vmem] + [any_space] * len(blocks),
        out_specs=in_vmem,
        scratch_shapes=[
            pltpu.VMEM((4,) + shape[:3] + (rows, shape[4]), bf16), pltpu.SemaphoreType.DMA((len(blocks),))
        ],
        compiler_params=kernel_room,
        cost_estimate=light,
    )(grads, *blocks)


def inner_kernel(n_seq, spot, own, other, order, slope_q, slope_p, inner_q, inner_p):
    found = jnp.concatenate([own[...], other[...]], axis=1)
    hidden = jnp.zeros_like(found)
    for _ in range(3):
        piece = found.astype(bf16)
        hidden = hidden + jnp.dot(piece, order[...], preferred_element_type=f32)
        found = found - piece.astype(f32)
    first_row = 0
    for slope, inner in ((slope_q, inner_q), (slope_p, inner_p)):
        row = lax.broadcasted_iota(jnp.int32, (slope.shape[0], 1), 0) + first_row
        spread_out = jnp.zeros(slope.shape, f32)
        for k in range(n_seq):
            inside = (row >= spot[head + k]) & (row < spot[head + n_seq + k])
            spread_out = jnp.where(inside, hidden[k : k + 1, :], spread_out)
        inner[...] = (slope[...] * spread_out).astype(bf16)
        first_row += slope.shape[0]


def inner_of(spot, own, other, order, slope_q, slope_p, n_seq):
    return pl.pallas_call(
        lambda *refs: inner_kernel(n_seq, *refs),
        out_shape=(jax.ShapeDtypeStruct(slope_q.shape, bf16), jax.ShapeDtypeStruct(slope_p.shape, bf16)),
        in_specs=[in_smem] + [in_vmem] * 5,
        out_specs=(in_vmem,) * 2,
        compiler_params=kernel_room,
        cost_estimate=light,
    )(spot, own, other, order, slope_q, slope_p)


def spread(block, axes, count):
    return lax.all_to_all(jnp.broadcast_to(block[None], (count,) + block.shape), axes, 0, 0)


def per_device(sizes, query_cache, passage_cache, positive, query_tokens, passage_tokens,
               query_lengths, passage_lengths, norm_gain, adapter_down, adapter_up):
    nx, nyl, nz, nyh, nc = sizes
    n_all = nx * nyl * nz * nyh * nc
    n_pb, n_pa = nx * nyl, nz * nyh * nc
    x_i, yl_i, z_i, yh_i, c_i = (lax.axis_index(a) for a in everyone)
    first_core = c_i == 0
    own_queries, own_passages = query_cache[0], passage_cache[0]
    width = own_queries.shape[1]
    qrow, prow = own_queries.shape[0], own_passages.shape[0]
    d_own, hidden_width = adapter_down.shape
    r_own = adapter_up.shape[0]
    q_seqs, p_seqs = query_lengths.shape[-1], passage_lengths.shape[-1]

    chips = ("x", "yl", "z", "yh")
    n_chips = n_all // nc
    gain = norm_gain.astype(f32)
    gained_down = (adapter_down.astype(f32) * gain[:, None]).astype(bf16)
    (q_next, p_next, gained_down, adapter_up, query_lengths, passage_lengths, yl_i, yh_i, c_i) = barrier(
        (swap(own_queries, "yh"), swap(own_passages, "yl"), gained_down, adapter_up,
         query_lengths, passage_lengths, yl_i, yh_i, c_i)
    )

    q_pair = jnp.concatenate([own_queries, q_next], axis=0)
    p_pair = jnp.concatenate([own_passages, p_next], axis=0)
    q_before, q_after = ring_sides(q_pair, "z")
    p_before, p_after = ring_sides(p_pair, "x")
    q_blocks = [q_pair, q_before, *ring_far(q_before, q_after, "z"), q_after]
    p_blocks = [p_pair, p_before, *ring_far(p_before, p_after, "x"), p_after]
    p_other = swap(p_pair, "c")

    tok_q, tok_p = query_tokens[0, 0], passage_tokens[0, 0]
    lengths = jnp.concatenate([query_lengths[0, 0], passage_lengths[0, 0]], axis=0)
    n_seq = lengths.shape[0]
    pad = -n_seq % 8
    n_seq8 = n_seq + pad
    ends = jnp.cumsum(lengths)
    spot = jnp.concatenate([jnp.stack([yl_i, yh_i, c_i, x_i, z_i]), ends - lengths, ends]).astype(jnp.int32)

    here = jnp.arange(hidden_width, dtype=jnp.int32)
    unit, rest = here % r_own, here // r_own
    yh_s, rest = rest % nyh, rest // nyh
    z_s, rest = rest % nz, rest // nz
    yl_s, rest = rest % nyl, rest // nyl
    x_s, c_s = lax.rem(x_i - rest % nx + nx, nx), lax.rem(c_i + rest // nx, nc)
    place = ((((x_s * nyl + yl_s) * nz + z_s) * nyh + yh_s) * nc + c_s) * r_own + unit
    order = (place[:, None] == here[None, :]).astype(bf16)

    q_blocks, p_blocks, p_other, spot, order, gained_down, adapter_up = barrier(
        (q_blocks, p_blocks, p_other, spot, order, gained_down, adapter_up)
    )
    near = spread(
        jnp.concatenate([gained_down, adapter_up.reshape(-1, hidden_width)], axis=0),
        ("yl", "z", "yh"), nyl * nz * nyh,
    ).reshape(nyl, nz, nyh, -1, hidden_width)
    p_blocks = barrier(p_blocks + [p_other] + [swap(b, "c") for b in p_blocks[1:]])

    scores, local_top, local_sum = score_block(q_blocks, p_blocks)

    m_i = z_i * nyh + yh_i
    groups = nz * nyh
    step = jnp.arange(groups, dtype=jnp.int32)
    owner = lax.rem(z_i - step // nyh + nz, nz) * nyh + lax.rem(yh_i - step % nyh + nyh, nyh)
    pick = owner[:, None] == step[None, :]

    def to_owner(v):
        return jnp.sum(jnp.where(pick[:, :, None], v.reshape(groups, 1, qrow), 0), axis=0)

    def to_step(v):
        return jnp.sum(jnp.where(pick[:, :, None], v.reshape(1, groups, qrow), 0), axis=1).reshape(-1)

    packet = jnp.concatenate(
        [to_owner(local_top).reshape(-1), to_owner(local_sum).reshape(-1), positive[0].astype(f32)]
    )
    packet = jnp.pad(packet, (0, -packet.shape[0] % 128))
    packet, near = barrier((packet, near))
    near_down, near_up = near[:, :, :, :d_own], near[:, :, :, d_own:]
    down_before, down_after = ring_sides(near_down, "x")
    up_before, up_after = ring_sides(near_up, "x")
    stats = spread(packet, ("z", "yh"), groups)

    stats, down_before, down_after = barrier((stats, down_before, down_after))
    down_far = ring_far(down_before, down_after, "x")
    n_q = groups * qrow
    tops, sums = stats[:, :n_q], stats[:, n_q : 2 * n_q]
    row_top = jnp.max(tops, axis=0)
    row_sum = jnp.sum(sums * jnp.exp(tops - row_top[None, :]), axis=0)
    target = stats[:, 2 * n_q : 2 * n_q + qrow]
    stat = jnp.stack([to_step(row_top), to_step(row_sum), to_step(target)], axis=1)

    core_step = jnp.arange(nc, dtype=jnp.int32)[:, None, None, None]
    x_step = jnp.arange(nx, dtype=jnp.int32)[None, :, None, None]
    yl_step = jnp.arange(nyl, dtype=jnp.int32)[None, None, :, None]
    lane = jnp.arange(prow, dtype=jnp.int32)[None, None, None, :]
    a_of = m_i * nc + lax.rem(c_i + core_step, nc)
    b_of = lax.rem(x_i - x_step + nx, nx) * nyl + lax.rem(yl_i - yl_step + nyl, nyl)
    columns = (a_of * (n_pb * prow) + b_of * prow + lane).reshape(-1)

    coupling, q_few, p_few = couple(
        spot, scores, stat, columns[None, :], q_blocks, p_blocks, sizes, (q_seqs, qrow, p_seqs, prow)
    )
    p_few = lax.all_to_all(p_few, ("x", "yl", "c"), 0, 0)
    q_few = lax.all_to_all(q_few, ("z", "yh"), 0, 0)

    q_part = grad_parts(coupling, p_blocks, nz, False)
    coupling, q_few, q_part, up_before, up_after = barrier((coupling, q_few, q_part, up_before, up_after))
    p_part = grad_parts(coupling, q_blocks, nc * nx, True)
    p_keep, p_give = p_part[:nx], p_part[nx:]

    p_few, p_keep, p_give, down_far, up_before, up_after, q_terms = barrier(
        (p_few, p_keep, p_give, down_far, up_before, up_after, ring_sum(q_part, "z", nz))
    )
    up_far = ring_far(up_before, up_after, "x")
    down_x = [near_down, down_before, *down_far, down_after]
    up_x = [near_up, up_before, *up_far, up_after]

    p_sum = core_add(p_keep, [swap(b, "c") for b in p_give])
    down_blocks, p_sum, up_x = barrier((down_x + [swap(b, "c") for b in down_x], p_sum, up_x))
    slope_q, slope_p, active_sums = token_half(spot, down_blocks, tok_q, tok_p, n_seq, n_seq8)
    r_block, d_block = hidden_width // n_pb, width // n_pa
    sum_blocks = active_sums.astype(bf16).reshape(n_seq8, n_pb, r_block).transpose(1, 0, 2)
    sum_blocks = jnp.pad(sum_blocks, ((0, 0), (0, 0), (0, -r_block % 128)))
    q_few = jnp.sum(q_few.astype(f32), axis=0).astype(bf16)
    p_few = jnp.sum(p_few.astype(f32), axis=0).astype(bf16)

    emb_grads = jnp.concatenate([q_few, p_few], axis=0).astype(f32)
    seq_grads = (emb_grads / lengths.astype(f32)[:, None]).astype(bf16)
    seq_grads = jnp.pad(seq_grads, ((0, pad), (0, 0)))

    grad_blocks = seq_grads.reshape(n_seq8, n_pa, d_block).transpose(1, 0, 2)
    packet = jnp.concatenate(
        [
            jnp.broadcast_to(grad_blocks[None], (n_pb,) + grad_blocks.shape),
            jnp.broadcast_to(sum_blocks[:, None], (n_pb, n_pa) + sum_blocks.shape[1:]),
        ],
        axis=-1,
    ).reshape(n_all, n_seq8, -1)

    seq_both = jnp.concatenate([seq_grads, swap(seq_grads, "c")], axis=0)
    p_terms = ring_sum(p_sum, "x", nx)

    hidden = hidden_of(seq_both, up_x, r_own * width // hidden_width, hidden_width // nc)
    inner_q, inner_p = inner_of(
        spot, hidden[:n_seq8], swap(hidden[n_seq8:], "c"), order, slope_q, slope_p, n_seq
    )
    inner_q, inner_p, p_terms, packet = barrier((inner_q, inner_p, p_terms, packet))
    everything = lax.all_to_all(packet, everyone, 0, 0).reshape(n_all * n_seq8, -1)
    q_own, q_away = ring_add(q_terms)
    p_own, p_away = ring_add(p_terms)
    keep, give = down_parts(spot, tok_q, tok_p, inner_q, inner_p, d_own)
    keep, give, q_own, q_away, p_own, p_away, everything = barrier(
        (keep, give, q_own, q_away, p_own, p_away, everything)
    )
    chip_sum = chip_add(keep, [swap(b, "c") for b in give])
    up_block = lax.dot_general(
        everything[:, d_block : d_block + r_block], everything[:, :d_block], turned, preferred_element_type=f32
    ).reshape(nz, nyh, nc, r_own, 1, d_block)

    def trade(block, axis, index):
        first = index == 0
        mine = jnp.where(first, block[..., 0, :, :, :], block[..., 1, :, :, :])
        theirs = swap(jnp.where(first, block[..., 1, :, :, :], block[..., 0, :, :, :]), axis)
        return jnp.concatenate(
            [jnp.where(first, mine, theirs), jnp.where(first, theirs, mine)], axis=-2
        )

    up_block = trade(trade(up_block, "c", c_i), "yh", yh_i)
    chip_sum, up_block = barrier((chip_sum, up_block))
    z_blocks = [lax.dynamic_index_in_dim(up_block, lax.rem(z_i + k, nz), 0, keepdims=False) for k in range(nz)]
    z_blocks = [z_blocks[0]] + [shift(z_blocks[k], "z", k, nz) for k in range(1, nz)]
    query_grad = (q_own + swap(q_away, "yh").astype(f32)).astype(bf16)
    passage_grad = (p_own + swap(p_away, "yl").astype(f32)).astype(bf16)
    arrived = lax.all_to_all(chip_sum, chips, 0, 0)

    up_grad = jnp.zeros((r_own, nz) + up_block.shape[2:], f32)
    for k in range(nz):
        up_grad = lax.dynamic_update_slice_in_dim(
            up_grad, z_blocks[k][:, None], lax.rem(z_i - k + nz, nz), axis=1
        )
    up_grad = up_grad.reshape(r_own, width)

    ungained = jnp.sum(arrived.astype(f32), axis=0)
    down_grad = ungained * gain[:, None]
    gain_grad = jnp.sum(ungained * adapter_down.astype(f32), axis=1)
    return (query_grad[None], passage_grad[None], down_grad, up_grad, gain_grad)


def solution(mesh):
    nyl, nyh, nc = 2, 2, 2
    nx, nz = mesh.shape["pb"] // nyl, mesh.shape["pa"] // (nyh * nc)
    sizes = (nx, nyl, nz, nyh, nc)
    fine = Mesh(mesh.devices.reshape(sizes), everyone)
    pb, pa = ("x", "yl"), ("z", "yh", "c")
    in_specs = (
        P(pb, pa, None),
        P(pa, pb, None),
        P(pb, pa),
        P(pb, pa, None, None),
        P(pa, pb, None, None),
        P(pb, pa, None),
        P(pa, pb, None),
        P(everyone),
        P(everyone, None),
        P(everyone, None),
    )
    out_specs = (P(pb, pa, None), P(pa, pb, None), P(everyone, None), P(everyone, None), P(everyone))

    def body(*args):
        return per_device(sizes, *args)

    return jax.shard_map(body, mesh=fine, in_specs=in_specs, out_specs=out_specs, check_vma=False)
```

```python
import jax
import jax.numpy as jnp
from jax import lax
from jax.experimental import pallas as pl
from jax.experimental.pallas import tpu as pltpu
from jax.sharding import Mesh, PartitionSpec as P

scale = 1.0 / 0.05
epsilon = 1e-06
bf16 = jnp.bfloat16
f32 = jnp.float32
everyone = ("x", "yl", "z", "yh", "c")
swap2 = [(0, 1), (1, 0)]
barrier = lax.optimization_barrier


def shift(value, axis, step, size):
    return lax.ppermute(value, axis, [(i, (i + step) % size) for i in range(size)])


def swap(value, axis):
    return lax.ppermute(value, axis, swap2)


def ring_sides(block, ring):
    return shift(block, ring, 1, 4), shift(block, ring, 3, 4)


def ring_far(before, after, ring):
    half = before.shape[0] // 2
    return shift(before[:half], ring, 1, 4), shift(after[half:], ring, 3, 4)


def ring_sum(parts, ring, size):
    return [parts[0]] + [shift(parts[k], ring, size - k, size) for k in range(1, size)]


def cut_rows(part, count):
    rows = part.shape[0] // count
    return [part[k * rows : (k + 1) * rows] for k in range(count)]


def add_up(terms):
    total = terms[0].astype(f32)
    for t in terms[1:]:
        total = total + t.astype(f32)
    return total


def pair_sum(total, pair):
    half = total.shape[0] // 2
    return (total[:half] + swap(total[half:].astype(bf16), pair).astype(f32)).astype(bf16)


gelu_root = 0.7978845608028654
gelu_cube = 0.044715
kernel_room = pltpu.CompilerParams(vmem_limit_bytes=60 * 1024 * 1024)
light = pl.CostEstimate(flops=0, bytes_accessed=0, transcendentals=0)
any_space = pl.BlockSpec(memory_space=pl.ANY)
in_vmem = pl.BlockSpec(memory_space=pltpu.VMEM)
in_smem = pl.BlockSpec(memory_space=pltpu.SMEM)


turned = (((0,), (0,)), ((), ()))
contract = (((1,), (1,)), ((), ()))


def load_blocks(parts, wholes, sems):
    copies, n = [], 0
    for blocks, whole in zip(parts, wholes):
        row = 0
        for block in blocks:
            copies.append(pltpu.make_async_copy(block, whole.at[pl.ds(row, block.shape[0])], sems.at[n]))
            row, n = row + block.shape[0], n + 1
    for c in copies:
        c.start()
    return copies


def wait_all(copies):
    for c in copies:
        c.wait()


def score_kernel(n_q, n_p, *refs):
    q_blocks, p_blocks = refs[:n_q], refs[n_q : n_q + n_p]
    scores, top, total, q_all, p_all, sems = refs[n_q + n_p :]
    wait_all(load_blocks((q_blocks, p_blocks), (q_all, p_all), sems))
    s = lax.dot_general(q_all[...], p_all[...], contract, preferred_element_type=f32) * scale
    scores[...] = s
    m = jnp.max(s, axis=1, keepdims=True)
    top[...] = m
    total[...] = jnp.sum(jnp.exp(s - m), axis=1, keepdims=True)


def rows_of(blocks):
    return sum(b.shape[0] for b in blocks)


def block_scratch(q_blocks, p_blocks):
    width = q_blocks[0].shape[1]
    return [
        pltpu.VMEM((rows_of(q_blocks), width), bf16),
        pltpu.VMEM((rows_of(p_blocks), width), bf16),
        pltpu.SemaphoreType.DMA((len(q_blocks) + len(p_blocks),)),
    ]


def score_block(q_blocks, p_blocks):
    n_q, n_p = rows_of(q_blocks), rows_of(p_blocks)
    column = jax.ShapeDtypeStruct((n_q, 1), f32)
    return pl.pallas_call(
        lambda *refs: score_kernel(len(q_blocks), len(p_blocks), *refs),
        out_shape=(jax.ShapeDtypeStruct((n_q, n_p), f32), column, column),
        in_specs=[any_space] * (len(q_blocks) + len(p_blocks)),
        out_specs=(in_vmem,) * 3,
        scratch_shapes=block_scratch(q_blocks, p_blocks),
        compiler_params=kernel_room,
        cost_estimate=light,
    )(*q_blocks, *p_blocks)


def couple_kernel(n_q, n_p, sizes, counts, spot, scores, stat, columns, *refs):
    q_blocks, p_blocks = refs[:n_q], refs[n_q : n_q + n_p]
    coupling, q_few, p_few, q_all, p_all, sems = refs[n_q + n_p :]
    copies = load_blocks((q_blocks, p_blocks), (q_all, p_all), sems)
    soft = jnp.exp(scores[...] - stat[:, 0:1]) / stat[:, 1:2]
    hit = (stat[:, 2:3].astype(jnp.int32) == columns[...]).astype(f32)
    link = (soft - hit).astype(bf16)
    coupling[...] = link
    wait_all(copies)
    rows, cols = link.shape
    nx, nyl, nz, nyh, nc = sizes
    yl, yh, core, x, z = (spot[k] for k in range(head))
    q_seqs, q_row, p_seqs, p_row = counts
    n_q_owners = q_few.shape[0]

    n_few = n_q_owners * q_seqs
    few_i = lax.broadcasted_iota(jnp.int32, (n_few, rows), 0)
    here = lax.broadcasted_iota(jnp.int32, (n_few, rows), 1)
    seq, owner = few_i % q_seqs, few_i // q_seqs
    step = (z - owner // nyh + nz) % nz * nyh + (yh - owner % nyh + nyh) % nyh
    pick = (here == step * q_row + seq).astype(bf16)
    first = jnp.dot(pick, link, preferred_element_type=f32).astype(bf16)
    found = jnp.dot(first, p_all[...], preferred_element_type=f32) * scale
    for k in range(n_q_owners):
        q_few[k] = found[k * q_seqs : (k + 1) * q_seqs].astype(bf16)

    n_few = p_few.shape[0] * p_seqs
    few_i = lax.broadcasted_iota(jnp.int32, (n_few, cols), 0)
    here = lax.broadcasted_iota(jnp.int32, (n_few, cols), 1)
    seq, owner = few_i % p_seqs, few_i // p_seqs
    x_step = (x - owner // (nyl * nc) + nx) % nx
    yl_step = (yl - owner // nc % nyl + nyl) % nyl
    core_step = (core - owner % nc + nc) % nc
    pick = (here == ((core_step * nx + x_step) * nyl + yl_step) * p_row + seq).astype(bf16)
    first = lax.dot_general(pick, link, contract, preferred_element_type=f32).astype(bf16)
    found = jnp.dot(first, q_all[...], preferred_element_type=f32) * scale
    for k in range(p_few.shape[0]):
        p_few[k] = found[k * p_seqs : (k + 1) * p_seqs].astype(bf16)


def couple(spot, scores, stat, columns, q_blocks, p_blocks, sizes, counts):
    n_q, n_p = scores.shape
    width = q_blocks[0].shape[1]
    q_seqs, q_row, p_seqs, p_row = counts
    return pl.pallas_call(
        lambda *refs: couple_kernel(len(q_blocks), len(p_blocks), sizes, counts, *refs),
        out_shape=(
            jax.ShapeDtypeStruct((n_q, n_p), bf16),
            jax.ShapeDtypeStruct((n_q // q_row, q_seqs, width), bf16),
            jax.ShapeDtypeStruct((n_p // p_row, p_seqs, width), bf16),
        ),
        in_specs=[in_smem] + [in_vmem] * 3 + [any_space] * (len(q_blocks) + len(p_blocks)),
        out_specs=[in_vmem] * 3,
        scratch_shapes=block_scratch(q_blocks, p_blocks),
        compiler_params=kernel_room,
        cost_estimate=light,
    )(spot, scores, stat, columns, *q_blocks, *p_blocks)


def ring_add_kernel(n, *refs):
    for k in range(2):
        terms, out = refs[k * n : (k + 1) * n], refs[2 * n + 2 * k : 2 * n + 2 * k + 2]
        total = terms[0][...].astype(f32)
        for r in terms[1:]:
            total = total + r[...].astype(f32)
        half = total.shape[0] // 2
        out[0][...] = total[:half]
        out[1][...] = total[half:].astype(bf16)


def ring_add(first, second):
    rows, width = first[0].shape
    n = len(first)
    tile = width // 4

    def cut(n):
        return pl.BlockSpec((n, tile), lambda i: (0, i))

    half = [jax.ShapeDtypeStruct((rows // 2, width), f32), jax.ShapeDtypeStruct((rows // 2, width), bf16)]
    return pl.pallas_call(
        lambda *refs: ring_add_kernel(n, *refs),
        grid=(4,),
        out_shape=half * 2,
        in_specs=[cut(rows)] * (2 * n),
        out_specs=[cut(rows // 2)] * 4,
        compiler_params=kernel_room,
        cost_estimate=pl.CostEstimate(
            flops=0, bytes_accessed=4 * rows * width * (n + 2), transcendentals=0
        ),
    )(*first, *second)


def core_add_kernel(n, *refs):
    for keep, came, out in zip(refs[:n], refs[n : 2 * n], refs[2 * n :]):
        out[...] = (keep[...].astype(f32) + came[...].astype(f32)).astype(bf16)


def core_add(keep, came):
    steps = 2
    width = keep[0].shape[-1]

    def cut(a):
        return pl.BlockSpec(a.shape[:-1] + (width // steps,), lambda i: (0,) * (a.ndim - 1) + (i,))

    return pl.pallas_call(
        lambda *refs: core_add_kernel(len(keep), *refs),
        grid=(steps,),
        out_shape=[jax.ShapeDtypeStruct(a.shape, bf16) for a in keep],
        in_specs=[cut(a) for a in (*keep, *came)],
        out_specs=[cut(a) for a in keep],
        compiler_params=kernel_room,
        cost_estimate=light,
    )(*keep, *came)


def chip_add_kernel(n, keep, *refs):
    out = refs[n]
    rows = refs[0].shape[0]
    for k in range(n):
        here = pl.ds(k * rows, rows)
        out[here] = (keep[here].astype(f32) + refs[k][...].astype(f32)).astype(bf16)


def chip_add(keep, came):
    steps = 2
    width = keep.shape[-1]

    def cut(a):
        return pl.BlockSpec(a.shape[:-1] + (width // steps,), lambda i: (0,) * (a.ndim - 1) + (i,))

    return pl.pallas_call(
        lambda *refs: chip_add_kernel(len(came), *refs),
        grid=(steps,),
        out_shape=jax.ShapeDtypeStruct(keep.shape, bf16),
        in_specs=[cut(keep)] + [cut(a) for a in came],
        out_specs=cut(keep),
        compiler_params=kernel_room,
        cost_estimate=light,
    )(keep, *came)


def parts_kernel(n_blocks, n_out, turn, coupling, *refs):
    blocks, outs = refs[:n_blocks], refs[n_blocks : n_blocks + n_out]
    link = coupling[...]
    rows = outs[0].shape[0]
    whole = jnp.concatenate([b[...] for b in blocks], axis=0)
    if turn:
        part = lax.dot_general(link, whole, turned, preferred_element_type=f32)
    else:
        part = jnp.dot(link, whole, preferred_element_type=f32)
    part = (part * scale).astype(bf16)
    for k in range(n_out):
        outs[k][...] = part[k * rows : (k + 1) * rows]


def grad_parts(coupling, blocks, n_out, turn):
    n_q, n_p = coupling.shape
    width = blocks[0].shape[1]
    tile = 2048
    rows = (n_p if turn else n_q) // n_out

    def cut(n):
        return pl.BlockSpec((n, tile), lambda i: (0, i))

    return pl.pallas_call(
        lambda *refs: parts_kernel(len(blocks), n_out, turn, *refs),
        grid=(width // tile,),
        out_shape=[jax.ShapeDtypeStruct((rows, width), bf16)] * n_out,
        in_specs=[pl.BlockSpec((n_q, n_p), lambda i: (0, 0))] + [cut(b.shape[0]) for b in blocks],
        out_specs=[cut(rows)] * n_out,
        compiler_params=kernel_room,
        cost_estimate=pl.CostEstimate(
            flops=2 * n_q * n_p * width, bytes_accessed=2 * (n_q + n_p) * width, transcendentals=0
        ),
    )(coupling, *blocks)


def down_kernel(core, tok_q, tok_p, inner_q, inner_p, keep, *gives):
    part = lax.dot_general(tok_p[...], inner_p[...], turned, preferred_element_type=f32)
    part = part + lax.dot_general(tok_q[...], inner_q[...], turned, preferred_element_type=f32)
    chips, rows, hidden = keep.shape
    part = part.astype(bf16).reshape(chips, 2, rows, hidden)
    first = core[2] == 0
    piece = pl.program_id(0) // (pl.num_programs(0) // len(gives))

    @pl.when(first)
    def _():
        keep[...] = part[:, 0]

    @pl.when(jnp.logical_not(first))
    def _():
        keep[...] = part[:, 1]

    for k, give in enumerate(gives):

        @pl.when((piece == k) & first)
        def _():
            give[...] = part[:, 1]

        @pl.when((piece == k) & jnp.logical_not(first))
        def _():
            give[...] = part[:, 0]


def down_parts(spot, tok_q, tok_p, inner_q, inner_p, rows):
    width, hidden = tok_q.shape[1], inner_q.shape[1]
    tile, pieces = 1024, 4
    chips = tile // (2 * rows)
    steps = width // tile
    each = steps // pieces
    n_chips = width // (2 * rows)

    def cut(a):
        return pl.BlockSpec((a.shape[0], tile), lambda i: (0, i))

    def piece_spec(k):
        return pl.BlockSpec((chips, rows, hidden), lambda i: (jnp.clip(i - k * each, 0, each - 1), 0, 0))

    out = pl.pallas_call(
        down_kernel,
        grid=(steps,),
        out_shape=[jax.ShapeDtypeStruct((n_chips, rows, hidden), bf16)]
        + [jax.ShapeDtypeStruct((n_chips // pieces, rows, hidden), bf16)] * pieces,
        in_specs=[
            in_smem, cut(tok_q), cut(tok_p),
            pl.BlockSpec(inner_q.shape, lambda i: (0, 0)), pl.BlockSpec(inner_p.shape, lambda i: (0, 0)),
        ],
        out_specs=[pl.BlockSpec((chips, rows, hidden), lambda i: (i, 0, 0))] + [piece_spec(k) for k in range(pieces)],
        compiler_params=kernel_room,
        cost_estimate=pl.CostEstimate(
            flops=2 * (tok_q.shape[0] + tok_p.shape[0]) * width * hidden, bytes_accessed=4 * width * hidden,
            transcendentals=0,
        ),
    )(spot, tok_q, tok_p, inner_q, inner_p)
    return out[0], out[1:]


ring_places = ((0, 0, 2), (1, 0, 2), (2, 0, 1), (2, 1, 1), (3, 0, 2))
head = 5


def token_kernel(n_seq, n_blocks, spot, *rest):
    blocks = rest[:n_blocks]
    tok_q, tok_p, slope_q, slope_p, sums, weights, sems = rest[n_blocks:]
    i = pl.program_id(0)

    @pl.when(i == 0)
    def _():
        copies = []
        for k in range(n_blocks):
            step, first, count = ring_places[k % len(ring_places)]
            x = lax.rem(spot[3] - step + 4, 4)
            core = lax.rem(spot[2] + k // len(ring_places), 2)
            copies.append(
                pltpu.make_async_copy(
                    blocks[k].at[:, :, :, pl.ds(0, weights.shape[5])],
                    weights.at[x, pl.ds(first, count), :, :, core],
                    sems.at[k],
                )
            )
        for c in copies:
            c.start()
        sums[...] = jnp.zeros_like(sums)
        for c in copies:
            c.wait()

    hidden = weights.shape[-1]

    def work(tok, slope, first_row):
        rows = tok.shape[0]
        wide = tok[...].astype(f32)
        inverse = lax.rsqrt(jnp.mean(wide * wide, axis=1, keepdims=True) + epsilon)
        pre = jnp.dot(tok[...], weights[...].reshape(-1, hidden), preferred_element_type=f32) * inverse
        square = pre * pre
        bend = jnp.tanh(gelu_root * pre * (1.0 + gelu_cube * square))
        up = 0.5 * (1.0 + bend)
        active = (pre * up).astype(bf16)
        steep = up + 0.5 * pre * (1.0 - bend * bend) * (gelu_root * (1.0 + 3.0 * gelu_cube * square))
        slope[...] = steep * inverse
        seq = lax.broadcasted_iota(jnp.int32, (sums.shape[0], rows), 0)
        row = lax.broadcasted_iota(jnp.int32, (sums.shape[0], rows), 1) + first_row
        member = jnp.zeros((sums.shape[0], rows), f32)
        for k in range(n_seq):
            inside = (row >= spot[head + k]) & (row < spot[head + n_seq + k]) & (seq == k)
            member = jnp.where(inside, 1.0, member)
        sums[...] += jnp.dot(member.astype(bf16), active, preferred_element_type=f32)

    @pl.when(i == 0)
    def _():
        work(tok_q, slope_q, 0)

    @pl.when(i > 0)
    def _():
        work(tok_p, slope_p, tok_q.shape[0] + (i - 1) * tok_p.shape[0])


def token_half(spot, blocks, tok_q, tok_p, n_seq, n_seq8):
    width = tok_q.shape[1]
    nyl, nz, nyh, both, hidden = blocks[0].shape
    d_own = width // (4 * nyl * nz * nyh * 2)
    steps = 2
    tile = tok_p.shape[0] // steps

    def tile_of(i):
        return (jnp.maximum(i - 1, 0), 0)

    return pl.pallas_call(
        lambda *refs: token_kernel(n_seq, len(blocks), *refs),
        grid=(steps + 1,),
        out_shape=(
            jax.ShapeDtypeStruct((tok_q.shape[0], hidden), f32),
            jax.ShapeDtypeStruct((tok_p.shape[0], hidden), f32),
            jax.ShapeDtypeStruct((n_seq8, hidden), f32),
        ),
        in_specs=[in_smem] + [any_space] * len(blocks)
        + [pl.BlockSpec(tok_q.shape, lambda i: (0, 0)), pl.BlockSpec((tile, width), tile_of)],
        out_specs=(
            pl.BlockSpec((tok_q.shape[0], hidden), lambda i: (0, 0)),
            pl.BlockSpec((tile, hidden), tile_of),
            pl.BlockSpec((n_seq8, hidden), lambda i: (0, 0)),
        ),
        scratch_shapes=[
            pltpu.VMEM((4, nyl, nz, nyh, 2, d_own, hidden), bf16), pltpu.SemaphoreType.DMA((len(blocks),))
        ],
        compiler_params=kernel_room,
        cost_estimate=light,
    )(spot, *blocks, tok_q, tok_p)


def hidden_kernel(n_blocks, units, grads, *refs):
    blocks = refs[:n_blocks]
    out, lines, sems = refs[n_blocks:]
    rows, line = lines.shape[-2:]
    copies = [
        pltpu.make_async_copy(
            blocks[k].at[:, :, :, pl.ds(blocks[k].shape[3] - rows, rows)],
            lines.at[step, pl.ds(first, count)],
            sems.at[k],
        )
        for k, (step, first, count) in enumerate(ring_places)
    ]
    for c in copies:
        c.start()
    n_seq, width = grads.shape
    per_unit = width // line
    cut = jnp.concatenate([grads[:, j * line : (j + 1) * line] for j in range(per_unit)], axis=0)
    for c in copies:
        c.wait()
    flat = lines[...].reshape(-1, line)
    found = lax.dot_general(cut, flat, contract, preferred_element_type=f32)
    which = lax.broadcasted_iota(jnp.int32, (n_seq, flat.shape[0]), 1) % per_unit
    kept = jnp.zeros((n_seq, flat.shape[0]), f32)
    for j in range(per_unit):
        kept = jnp.where(which == j, found[j * n_seq : (j + 1) * n_seq], kept)
    source = lax.broadcasted_iota(jnp.int32, (flat.shape[0], units), 0) // per_unit
    to = lax.broadcasted_iota(jnp.int32, (flat.shape[0], units), 1)
    gather = (source == to).astype(bf16)
    total = jnp.zeros((n_seq, units), f32)
    for _ in range(3):
        piece = kept.astype(bf16)
        total = total + jnp.dot(piece, gather, preferred_element_type=f32)
        kept = kept - piece.astype(f32)
    out[...] = total


def hidden_of(grads, blocks, rows, units):
    shape = blocks[0].shape
    return pl.pallas_call(
        lambda *refs: hidden_kernel(len(blocks), units, *refs),
        out_shape=jax.ShapeDtypeStruct((grads.shape[0], units), f32),
        in_specs=[in_vmem] + [any_space] * len(blocks),
        out_specs=in_vmem,
        scratch_shapes=[
            pltpu.VMEM((4,) + shape[:3] + (rows, shape[4]), bf16), pltpu.SemaphoreType.DMA((len(blocks),))
        ],
        compiler_params=kernel_room,
        cost_estimate=light,
    )(grads, *blocks)


def inner_kernel(n_seq, spot, own, other, order, slope_q, slope_p, inner_q, inner_p):
    found = jnp.concatenate([own[...], other[...]], axis=1)
    hidden = jnp.zeros_like(found)
    for _ in range(3):
        piece = found.astype(bf16)
        hidden = hidden + jnp.dot(piece, order[...], preferred_element_type=f32)
        found = found - piece.astype(f32)
    first_row = 0
    for slope, inner in ((slope_q, inner_q), (slope_p, inner_p)):
        row = lax.broadcasted_iota(jnp.int32, (slope.shape[0], 1), 0) + first_row
        spread_out = jnp.zeros(slope.shape, f32)
        for k in range(n_seq):
            inside = (row >= spot[head + k]) & (row < spot[head + n_seq + k])
            spread_out = jnp.where(inside, hidden[k : k + 1, :], spread_out)
        inner[...] = (slope[...] * spread_out).astype(bf16)
        first_row += slope.shape[0]


def inner_of(spot, own, other, order, slope_q, slope_p, n_seq):
    return pl.pallas_call(
        lambda *refs: inner_kernel(n_seq, *refs),
        out_shape=(jax.ShapeDtypeStruct(slope_q.shape, bf16), jax.ShapeDtypeStruct(slope_p.shape, bf16)),
        in_specs=[in_smem] + [in_vmem] * 5,
        out_specs=(in_vmem,) * 2,
        compiler_params=kernel_room,
        cost_estimate=light,
    )(spot, own, other, order, slope_q, slope_p)


def spread(block, axes, count):
    return lax.all_to_all(jnp.broadcast_to(block[None], (count,) + block.shape), axes, 0, 0)


def per_device(sizes, query_cache, passage_cache, positive, query_tokens, passage_tokens,
               query_lengths, passage_lengths, norm_gain, adapter_down, adapter_up):
    nx, nyl, nz, nyh, nc = sizes
    n_all = nx * nyl * nz * nyh * nc
    n_pb, n_pa = nx * nyl, nz * nyh * nc
    x_i, yl_i, z_i, yh_i, c_i = (lax.axis_index(a) for a in everyone)
    first_core = c_i == 0
    own_queries, own_passages = query_cache[0], passage_cache[0]
    width = own_queries.shape[1]
    qrow, prow = own_queries.shape[0], own_passages.shape[0]
    d_own, hidden_width = adapter_down.shape
    r_own = adapter_up.shape[0]
    q_seqs, p_seqs = query_lengths.shape[-1], passage_lengths.shape[-1]

    chips = ("x", "yl", "z", "yh")
    n_chips = n_all // nc
    gain = norm_gain.astype(f32)
    gained_down = (adapter_down.astype(f32) * gain[:, None]).astype(bf16)
    (q_next, p_next, gained_down, adapter_up, query_lengths, passage_lengths, yl_i, yh_i, c_i) = barrier(
        (swap(own_queries, "yh"), swap(own_passages, "yl"), gained_down, adapter_up,
         query_lengths, passage_lengths, yl_i, yh_i, c_i)
    )

    q_pair = jnp.concatenate([own_queries, q_next], axis=0)
    p_pair = jnp.concatenate([own_passages, p_next], axis=0)
    q_before, q_after = ring_sides(q_pair, "z")
    p_before, p_after = ring_sides(p_pair, "x")
    q_blocks = [q_pair, q_before, *ring_far(q_before, q_after, "z"), q_after]
    p_blocks = [p_pair, p_before, *ring_far(p_before, p_after, "x"), p_after]
    p_other = swap(p_pair, "c")

    tok_q, tok_p = query_tokens[0, 0], passage_tokens[0, 0]
    lengths = jnp.concatenate([query_lengths[0, 0], passage_lengths[0, 0]], axis=0)
    n_seq = lengths.shape[0]
    pad = -n_seq % 8
    n_seq8 = n_seq + pad
    ends = jnp.cumsum(lengths)
    spot = jnp.concatenate([jnp.stack([yl_i, yh_i, c_i, x_i, z_i]), ends - lengths, ends]).astype(jnp.int32)

    here = jnp.arange(hidden_width, dtype=jnp.int32)
    unit, rest = here % r_own, here // r_own
    yh_s, rest = rest % nyh, rest // nyh
    z_s, rest = rest % nz, rest // nz
    yl_s, rest = rest % nyl, rest // nyl
    x_s, c_s = lax.rem(x_i - rest % nx + nx, nx), lax.rem(c_i + rest // nx, nc)
    place = ((((x_s * nyl + yl_s) * nz + z_s) * nyh + yh_s) * nc + c_s) * r_own + unit
    order = (place[:, None] == here[None, :]).astype(bf16)

    q_blocks, p_blocks, p_other, spot, order, gained_down, adapter_up = barrier(
        (q_blocks, p_blocks, p_other, spot, order, gained_down, adapter_up)
    )
    near = spread(
        jnp.concatenate([gained_down, adapter_up.reshape(-1, hidden_width)], axis=0),
        ("yl", "z", "yh"), nyl * nz * nyh,
    ).reshape(nyl, nz, nyh, -1, hidden_width)
    p_blocks = barrier(p_blocks + [p_other] + [swap(b, "c") for b in p_blocks[1:]])

    scores, local_top, local_sum = score_block(q_blocks, p_blocks)

    m_i = z_i * nyh + yh_i
    groups = nz * nyh
    step = jnp.arange(groups, dtype=jnp.int32)
    owner = lax.rem(z_i - step // nyh + nz, nz) * nyh + lax.rem(yh_i - step % nyh + nyh, nyh)
    pick = owner[:, None] == step[None, :]

    def to_owner(v):
        return jnp.sum(jnp.where(pick[:, :, None], v.reshape(groups, 1, qrow), 0), axis=0)

    def to_step(v):
        return jnp.sum(jnp.where(pick[:, :, None], v.reshape(1, groups, qrow), 0), axis=1).reshape(-1)

    packet = jnp.concatenate(
        [to_owner(local_top).reshape(-1), to_owner(local_sum).reshape(-1), positive[0].astype(f32)]
    )
    packet = jnp.pad(packet, (0, -packet.shape[0] % 128))
    packet, near = barrier((packet, near))
    near_down, near_up = near[:, :, :, :d_own], near[:, :, :, d_own:]
    down_before, down_after = ring_sides(near_down, "x")
    up_before, up_after = ring_sides(near_up, "x")
    stats = spread(packet, ("z", "yh"), groups)

    stats, down_before, down_after = barrier((stats, down_before, down_after))
    down_far = ring_far(down_before, down_after, "x")
    n_q = groups * qrow
    tops, sums = stats[:, :n_q], stats[:, n_q : 2 * n_q]
    row_top = jnp.max(tops, axis=0)
    row_sum = jnp.sum(sums * jnp.exp(tops - row_top[None, :]), axis=0)
    target = stats[:, 2 * n_q : 2 * n_q + qrow]
    stat = jnp.stack([to_step(row_top), to_step(row_sum), to_step(target)], axis=1)

    core_step = jnp.arange(nc, dtype=jnp.int32)[:, None, None, None]
    x_step = jnp.arange(nx, dtype=jnp.int32)[None, :, None, None]
    yl_step = jnp.arange(nyl, dtype=jnp.int32)[None, None, :, None]
    lane = jnp.arange(prow, dtype=jnp.int32)[None, None, None, :]
    a_of = m_i * nc + lax.rem(c_i + core_step, nc)
    b_of = lax.rem(x_i - x_step + nx, nx) * nyl + lax.rem(yl_i - yl_step + nyl, nyl)
    columns = (a_of * (n_pb * prow) + b_of * prow + lane).reshape(-1)

    coupling, q_few, p_few = couple(
        spot, scores, stat, columns[None, :], q_blocks, p_blocks, sizes, (q_seqs, qrow, p_seqs, prow)
    )
    p_few = lax.all_to_all(p_few, ("x", "yl", "c"), 0, 0)
    q_few = lax.all_to_all(q_few, ("z", "yh"), 0, 0)

    q_part = grad_parts(coupling, p_blocks, nz, False)
    coupling, q_few, q_part, up_before, up_after = barrier((coupling, q_few, q_part, up_before, up_after))
    p_part = grad_parts(coupling, q_blocks, nc * nx, True)
    p_keep, p_give = p_part[:nx], p_part[nx:]

    p_few, p_keep, p_give, down_far, up_before, up_after, q_terms = barrier(
        (p_few, p_keep, p_give, down_far, up_before, up_after, ring_sum(q_part, "z", nz))
    )
    up_far = ring_far(up_before, up_after, "x")
    down_x = [near_down, down_before, *down_far, down_after]
    up_x = [near_up, up_before, *up_far, up_after]

    p_sum = core_add(p_keep, [swap(b, "c") for b in p_give])
    down_blocks, p_sum, up_x = barrier((down_x + [swap(b, "c") for b in down_x], p_sum, up_x))
    slope_q, slope_p, active_sums = token_half(spot, down_blocks, tok_q, tok_p, n_seq, n_seq8)
    r_block, d_block = hidden_width // n_pb, width // n_pa
    sum_blocks = active_sums.astype(bf16).reshape(n_seq8, n_pb, r_block).transpose(1, 0, 2)
    sum_blocks = jnp.pad(sum_blocks, ((0, 0), (0, 0), (0, -r_block % 128)))
    q_few = jnp.sum(q_few.astype(f32), axis=0).astype(bf16)
    p_few = jnp.sum(p_few.astype(f32), axis=0).astype(bf16)

    emb_grads = jnp.concatenate([q_few, p_few], axis=0).astype(f32)
    seq_grads = (emb_grads / lengths.astype(f32)[:, None]).astype(bf16)
    seq_grads = jnp.pad(seq_grads, ((0, pad), (0, 0)))

    grad_blocks = seq_grads.reshape(n_seq8, n_pa, d_block).transpose(1, 0, 2)
    packet = jnp.concatenate(
        [
            jnp.broadcast_to(grad_blocks[None], (n_pb,) + grad_blocks.shape),
            jnp.broadcast_to(sum_blocks[:, None], (n_pb, n_pa) + sum_blocks.shape[1:]),
        ],
        axis=-1,
    ).reshape(n_all, n_seq8, -1)

    seq_both = jnp.concatenate([seq_grads, swap(seq_grads, "c")], axis=0)
    p_terms = ring_sum(p_sum, "x", nx)

    hidden = hidden_of(seq_both, up_x, r_own * width // hidden_width, hidden_width // nc)
    inner_q, inner_p = inner_of(
        spot, hidden[:n_seq8], swap(hidden[n_seq8:], "c"), order, slope_q, slope_p, n_seq
    )
    inner_q, inner_p, p_terms, packet = barrier((inner_q, inner_p, p_terms, packet))
    everything = lax.all_to_all(packet, everyone, 0, 0).reshape(n_all * n_seq8, -1)
    q_own, q_away, p_own, p_away = ring_add(q_terms, p_terms)
    keep, give = down_parts(spot, tok_q, tok_p, inner_q, inner_p, d_own)
    keep, give, q_own, q_away, p_own, p_away, everything = barrier(
        (keep, give, q_own, q_away, p_own, p_away, everything)
    )
    chip_sum = chip_add(keep, [swap(b, "c") for b in give])
    up_block = lax.dot_general(
        everything[:, d_block : d_block + r_block], everything[:, :d_block], turned, preferred_element_type=f32
    ).reshape(nz, nyh, nc, r_own, 1, d_block)

    def trade(block, axis, index):
        first = index == 0
        mine = jnp.where(first, block[..., 0, :, :, :], block[..., 1, :, :, :])
        theirs = swap(jnp.where(first, block[..., 1, :, :, :], block[..., 0, :, :, :]), axis)
        return jnp.concatenate(
            [jnp.where(first, mine, theirs), jnp.where(first, theirs, mine)], axis=-2
        )

    up_block = trade(trade(up_block, "c", c_i), "yh", yh_i)
    chip_sum, up_block = barrier((chip_sum, up_block))
    z_blocks = [lax.dynamic_index_in_dim(up_block, lax.rem(z_i + k, nz), 0, keepdims=False) for k in range(nz)]
    z_blocks = [z_blocks[0]] + [shift(z_blocks[k], "z", k, nz) for k in range(1, nz)]
    query_grad = (q_own + swap(q_away, "yh").astype(f32)).astype(bf16)
    passage_grad = (p_own + swap(p_away, "yl").astype(f32)).astype(bf16)
    arrived = lax.all_to_all(chip_sum, chips, 0, 0)

    up_grad = jnp.zeros((r_own, nz) + up_block.shape[2:], f32)
    for k in range(nz):
        up_grad = lax.dynamic_update_slice_in_dim(
            up_grad, z_blocks[k][:, None], lax.rem(z_i - k + nz, nz), axis=1
        )
    up_grad = up_grad.reshape(r_own, width)

    ungained = jnp.sum(arrived.astype(f32), axis=0)
    down_grad = ungained * gain[:, None]
    gain_grad = jnp.sum(ungained * adapter_down.astype(f32), axis=1)
    return (query_grad[None], passage_grad[None], down_grad, up_grad, gain_grad)


def solution(mesh):
    nyl, nyh, nc = 2, 2, 2
    nx, nz = mesh.shape["pb"] // nyl, mesh.shape["pa"] // (nyh * nc)
    sizes = (nx, nyl, nz, nyh, nc)
    fine = Mesh(mesh.devices.reshape(sizes), everyone)
    pb, pa = ("x", "yl"), ("z", "yh", "c")
    in_specs = (
        P(pb, pa, None),
        P(pa, pb, None),
        P(pb, pa),
        P(pb, pa, None, None),
        P(pa, pb, None, None),
        P(pb, pa, None),
        P(pa, pb, None),
        P(everyone),
        P(everyone, None),
        P(everyone, None),
    )
    out_specs = (P(pb, pa, None), P(pa, pb, None), P(everyone, None), P(everyone, None), P(everyone))

    def body(*args):
        return per_device(sizes, *args)

    return jax.shard_map(body, mesh=fine, in_specs=in_specs, out_specs=out_specs, check_vma=False)
```
